512 devices in a mesh: dp: 4 (over y), row: 16 (over x, z_hi), col: 8 (over z_lo, core).
Axes of the slice: x: 4, y: 4, z: 16 (z_hi: 4, z_lo: 4; z = z_hi * 4 + z_lo), core: 2. Of those that a mesh axis runs over, the one named last changes fastest.
Arguments:
- activations: bfloat16 [7168, 6144], P(('dp', 'row'), 'col'), may hold values from -6 to 6
- cotangent: bfloat16 [7168, 12288], P(('dp', 'col'), 'row'), may hold values from -6 to 6
- preact: bfloat16 [7168, 12288], P(('dp', 'col'), 'row'), may hold values from -6 to 6
- weight: bfloat16 [6144, 12288], P('col', 'row'), may hold values from -0.078125 to 0.078125
- adapter_input_weight: bfloat16 [3, 32, 6144], P(None, None, 'col'), may hold values from -0.078125 to 0.078125
- adapter_output_weight: bfloat16 [3, 32, 12288], P(None, None, 'row'), may hold values from -1 to 1
- owner: int32 [4], replicated, may hold values from 0 to 2, as said below
Outputs:
- grad_input: bfloat16 [7168, 6144], P(('dp', 'row'), 'col')
- grad_weight: bfloat16 [6144, 12288], P('col', 'row')
- lora_in_grad: float32 [3, 32, 6144], P(None, None, 'col')
- lora_out_grad: float32 [3, 32, 12288], P(None, None, 'row')
The draws below stay inside these ranges and needn't reach their ends.
Inputs may be any that keep to these rules, and one draw needn't show every extreme that they name: `owner`: customer of each index of dp; each of the 3 customers owns at least one index, so some own several.
All inputs are finite; a program needn't handle non-finite values.
Results may differ from the reference program's by a relative error of at most 0.024.
Values may be sent and summed in bfloat16 or wider, within the bound.
A program may use at most 64 MiB of HBM per device.

```python
import jax
import jax.numpy as jnp
from jax import lax

MODEL_WIDTH = 6144
HIDDEN_HALF = 12288
ADAPTER_RANK = 32
CUSTOMER_COUNT = 3
TOK_GROUP = 1792
TOKENS = 7168
N_DP = 4
N_ROW = 16


def draw_owner(key, part):
    key = jax.random.fold_in(key, 7)
    return (jax.random.permutation(key, N_DP) % CUSTOMER_COUNT).astype(jnp.int32)


def block_scale(stream_key, dims, shards, least, top_value):
    loudness = 1.0
    for dim, parts in shards:
        heights = jax.random.uniform(jax.random.fold_in(jax.random.fold_in(stream_key, 6), dim), (parts,), jnp.float32, least / len(shards), top_value / len(shards))
        loudness = loudness * jnp.repeat(jnp.exp(heights), dims[dim] // parts).reshape((-1,) + (1,) * (len(dims) - 1 - dim))
    return loudness


def normal_values(stream_key, extent, deviation, bound, pieces=(), kind=jnp.bfloat16):
    factor_of = block_scale(stream_key, extent, pieces, -0.22, 0.18) if pieces else 1.0
    entries = jax.random.normal(stream_key, extent, jnp.float32) * deviation * factor_of
    return jnp.minimum(jnp.maximum(entries, -bound), bound).astype(kind)


def setup_inputs(seed: int = 0) -> dict:
    seeds = jax.random.split(jax.random.key(seed), 8)
    return {
        "activations": normal_values(seeds[0], (TOKENS, MODEL_WIDTH), 1.0, 6.0, ((0, 64), (1, 8))),
        "cotangent": normal_values(seeds[1], (TOKENS, HIDDEN_HALF), 1.0, 6.0, ((0, 32), (1, 16))),
        "preact": normal_values(seeds[2], (TOKENS, HIDDEN_HALF), 1.0, 6.0, ((0, 32), (1, 16))),
        "weight": normal_values(seeds[3], (MODEL_WIDTH, HIDDEN_HALF), MODEL_WIDTH ** -0.5, 0.078125, ((0, 8), (1, 16))),
        "adapter_input_weight": normal_values(seeds[4], (CUSTOMER_COUNT, ADAPTER_RANK, MODEL_WIDTH), MODEL_WIDTH ** -0.5, 0.078125, ((2, 8),)),
        "adapter_output_weight": normal_values(seeds[5], (CUSTOMER_COUNT, ADAPTER_RANK, HIDDEN_HALF), ADAPTER_RANK ** -0.5, 1.0, ((2, 16),)),
        "owner": draw_owner(jax.random.fold_in(seeds[7], 71), 0),
    }


adapter_scale_factor = 2.0


def gelu_slope(value):
    return 0.5 * (1.0 + lax.erf(value * 0.7071067811865476)) + value * jnp.exp(-0.5 * value * value) * 0.3989422804014327


def rounded(value):
    return lax.optimization_barrier(value.astype(jnp.bfloat16)).astype(jnp.float32)


def reference(activations, cotangent, preact, weight, adapter_input_weight, adapter_output_weight, owner):
    block_width = HIDDEN_HALF // N_ROW
    grad_pre = (cotangent.astype(jnp.float32) * gelu_slope(preact.astype(jnp.float32))).astype(jnp.bfloat16)
    weight_total = jnp.zeros((MODEL_WIDTH, HIDDEN_HALF), jnp.float32)
    in_total = jnp.zeros((CUSTOMER_COUNT, ADAPTER_RANK, MODEL_WIDTH), jnp.float32)
    out_total = jnp.zeros((CUSTOMER_COUNT, ADAPTER_RANK, HIDDEN_HALF), jnp.float32)
    outputs_list = []
    for group_index in range(N_DP):
        first = group_index * TOK_GROUP
        grouped_activation_rows = activations[first:first + TOK_GROUP]
        grouped_gradient_rows = grad_pre[first:first + TOK_GROUP]
        client_index = owner[group_index]
        rank_down_result = adapter_input_weight[client_index]
        rank_upward_result = adapter_output_weight[client_index]
        wide_down_result = rank_down_result.astype(jnp.float32)
        weight_total = weight_total + rounded(jnp.dot(grouped_activation_rows.T, grouped_gradient_rows, preferred_element_type=jnp.float32))
        rank_activation = jnp.dot(grouped_activation_rows, rank_down_result.T, preferred_element_type=jnp.float32).astype(jnp.bfloat16)
        low_sum = jnp.zeros((TOK_GROUP, ADAPTER_RANK), jnp.float32)
        input_sum = jnp.zeros((TOK_GROUP, MODEL_WIDTH), jnp.float32)
        for row_block in range(N_ROW):
            lower = row_block * block_width
            grad_piece = grouped_gradient_rows[:, lower:lower + block_width]
            rank_portion = jnp.dot(grad_piece, rank_upward_result[:, lower:lower + block_width].T, preferred_element_type=jnp.float32)
            incomplete_term = jnp.dot(grad_piece, weight[:, lower:lower + block_width].T, preferred_element_type=jnp.float32)
            incomplete_term = incomplete_term + adapter_scale_factor * jnp.dot(rank_portion, wide_down_result, precision=lax.Precision.HIGHEST)
            input_sum = input_sum + rounded(incomplete_term)
            low_sum = low_sum + rounded(rank_portion)
        outputs_list.append(input_sum.astype(jnp.bfloat16))
        rank_gradient = low_sum.astype(jnp.bfloat16)
        owner_mask = (jnp.arange(CUSTOMER_COUNT) == client_index).astype(jnp.float32)
        input_adapter_term = adapter_scale_factor * jnp.dot(rank_gradient.T, grouped_activation_rows, preferred_element_type=jnp.float32)
        output_adapter_term = adapter_scale_factor * jnp.dot(rank_activation.T, grouped_gradient_rows, preferred_element_type=jnp.float32)
        in_total = in_total + owner_mask[:, None, None] * input_adapter_term[None]
        out_total = out_total + owner_mask[:, None, None] * output_adapter_term[None]
    grad_input = jnp.concatenate(outputs_list, axis=0)
    return grad_input, weight_total.astype(jnp.bfloat16), in_total, out_total
```

```python
import functools

import jax
import jax.numpy as jnp
from jax import lax
from jax.experimental import pallas as pl
from jax.experimental.pallas import tpu as pltpu
from jax.sharding import PartitionSpec as P

MESH = pl.DeviceIdType.MESH
F32, BF16 = jnp.float32, jnp.bfloat16
SCALE = 2.0
CUSTOMERS = 3
RANK = 32


def gelu_slope(v):
    return 0.5 * (1.0 + lax.erf(v * 0.7071067811865476)) + v * jnp.exp(
        -0.5 * v * v
    ) * 0.3989422804014327


def kernel(
    x_in, cot_in, pre_in, w_in, ain_in, aout_in, owner,
    gi_out, gw_out, li_out, lo_out,
    gb, xb, cotv, prev, wv, av, bv, asel, bsel, weff, pb, rx, sz, rz, giv,
    wb, ry, ow, lis, lir, lot, lor, li2, li2r, lo2, lo2r, li3, lo3, lg, liv, lov,
    load_sem, store_sem, xz_s, xz_r, xx_s, xx_r, g_s, g_r, gk_s, gk_r, p_s, p_r, rz_s, rz_r,
    ry_s, ry_r, ag_s, ag_r, l_s, l_r,
):
    y, r, c = lax.axis_index("dp"), lax.axis_index("row"), lax.axis_index("col")
    i, j, o, k = r // 4, r % 4, c // 2, c % 2
    tok = xb.shape[1]
    blk = gb.shape[1]

    def at_x(s):
        return (y, ((i + s) % 4) * 4 + j, c)

    def at_zhi(s):
        return (y, i * 4 + (j + s) % 4, c)

    def at_zlo(s):
        return (y, r, ((o + s) % 4) * 2 + k)

    def at_y(s):
        return ((y + s) % 4, r, c)

    sibling = (y, r, o * 2 + 1 - k)

    def remote(src, dst, ss, rs, dev):
        return pltpu.make_async_remote_copy(
            src_ref=src, dst_ref=dst, send_sem=ss, recv_sem=rs, device_id=dev, device_id_type=MESH
        )

    loads = [
        pltpu.make_async_copy(a, b, load_sem.at[n])
        for n, (a, b) in enumerate(
            [(x_in, xb.at[r]), (cot_in, cotv), (pre_in, prev), (w_in, wv), (ain_in, av), (aout_in, bv)]
        )
    ]
    for cp in loads:
        cp.start()

    barrier = pltpu.get_barrier_semaphore()
    for s in range(1, 4):
        for dev in (at_x(s), at_zhi(s), at_zlo(s), at_y(s)):
            pl.semaphore_signal(barrier, inc=1, device_id=dev, device_id_type=MESH)
    pl.semaphore_signal(barrier, inc=1, device_id=sibling, device_id_type=MESH)
    pl.semaphore_wait(barrier, 13)

    def x_over_z(s):
        return remote(xb.at[r], xb.at[r], xz_s.at[s - 1], xz_r.at[s - 1], at_zhi(s))

    def x_over_x(jj, rel, s):
        row = i * 4 + jj
        return remote(xb.at[row], xb.at[row], xx_s.at[rel, s - 1], xx_r.at[rel, s - 1], at_x(s))

    loads[0].wait()
    for s in range(1, 4):
        x_over_z(s).start()
    for s in range(1, 4):
        x_over_x(j, 0, s).start()

    loads[1].wait()
    loads[2].wait()
    half = blk // 2
    for h in range(2):
        rows = pl.ds(h * half, half)
        v = prev[rows, :].astype(F32)
        gb[c, rows, :] = (cotv[rows, :].astype(F32) * gelu_slope(v)).astype(BF16)

    def g_over_z(s):
        return remote(gb.at[c], gb.at[c], g_s.at[s - 1], g_r.at[s - 1], at_zlo(s))

    def g_to_sibling(oo, rel):
        b = oo * 2 + k
        return remote(gb.at[b], gb.at[b], gk_s.at[rel], gk_r.at[rel], sibling)

    for s in range(1, 4):
        g_over_z(s).start()
    g_to_sibling(o, 0).start()

    loads[4].wait()
    loads[5].wait()
    mine = owner[y]
    a_sum = jnp.zeros(asel.shape, F32)
    b_sum = jnp.zeros(bsel.shape, F32)
    for n in range(CUSTOMERS):
        a_sum = a_sum + jnp.where(mine == n, av[n].astype(F32), 0.0)
        b_sum = b_sum + jnp.where(mine == n, bv[n].astype(F32), 0.0)
    asel[...] = a_sum.astype(BF16)
    bsel[...] = b_sum.astype(BF16)
    loads[3].wait()
    fold = lax.dot_general(asel[...], bsel[...], (((0,), (0,)), ((), ())), preferred_element_type=F32)
    weff[...] = (wv[...].astype(F32) + SCALE * fold).astype(BF16)

    def p_send(oo, kk, rel):
        rows = pl.ds(kk * blk, blk)
        return remote(
            pb.at[oo * 2 + kk], rx.at[i, rows], p_s.at[rel, kk], p_r.at[rel, kk],
            (y, oo * 4 + j, c),
        )

    def part(oo, kk):
        b = oo * 2 + kk
        pb[b] = lax.dot_general(
            gb[b], weff[...], (((1,), (1,)), ((), ())), preferred_element_type=F32
        ).astype(BF16)

        @pl.when(oo != i)
        def _():
            p_send(oo, kk, (oo - i + 4) % 4).start()

    part(o, k)
    g_to_sibling(o, 0).wait_recv()
    part(o, 1 - k)

    def step(s, carry):
        jj = (j - s + 4) % 4
        oo = (o - s + 4) % 4
        x_over_z(s).wait_recv()
        for t in range(1, 4):
            x_over_x(jj, s, t).start()
        g_over_z(s).wait_recv()
        g_to_sibling(oo, s).start()
        part(oo, k)
        g_to_sibling(oo, s).wait_recv()
        part(oo, 1 - k)
        return carry

    lax.fori_loop(1, 4, step, 0)

    for rel in range(4):
        for s in range(1, 4):
            x_over_x(j, rel, s).wait_recv()

    def ry_send(s):
        yy = (y + s) % 4
        return remote(wb.at[yy], ry.at[s - 1], ry_s.at[s - 1], ry_r.at[s - 1], at_y(s))

    width = weff.shape[0]
    xs = xb[...].reshape(16 * tok, width)
    gs = gb[...].reshape(8 * blk, width)
    for h in range(2):
        cols = width // 2
        term = lax.dot_general(
            xs[:, h * cols : (h + 1) * cols], gs, (((0,), (0,)), ((), ())), preferred_element_type=F32
        ).astype(BF16)
        wb[2 * h] = term[: cols // 2]
        wb[2 * h + 1] = term[cols // 2 :]
    for s in range(1, 4):
        ry_send(s).start()

    for rel in range(1, 4):
        for kk in range(2):
            p_send(o, kk, rel).wait_recv()
    for q in range(4):
        rows = pl.ds(q * tok, tok)
        total = pb[2 * i + q // 2, pl.ds((q % 2) * tok, tok), :].astype(F32)
        for s in range(1, 4):
            total = total + rx[(i + s) % 4, rows, :].astype(F32)
        sz[q] = total.astype(BF16)

    def rz_send(s):
        jj = (j + s) % 4
        return remote(sz.at[jj], rz.at[s - 1], rz_s.at[s - 1], rz_r.at[s - 1], at_zhi(s))

    for s in range(1, 4):
        rz_send(s).start()

    wfull = wb[...].reshape(width, width)
    lin = SCALE * lax.dot_general(bsel[...], wfull, (((1,), (1,)), ((), ())), preferred_element_type=F32)
    lout = SCALE * lax.dot_general(asel[...], wfull, (((1,), (0,)), ((), ())), preferred_element_type=F32)
    lis[...] = lin.reshape(lis.shape)
    lot[...] = lout.reshape(lot.shape)

    def li_x(s):
        return remote(lis.at[(i + s) % 4], lir.at[s - 1], l_s.at[0, s - 1], l_r.at[0, s - 1], at_x(s))

    def lo_z(s):
        return remote(lot.at[(o + s) % 4], lor.at[s - 1], l_s.at[1, s - 1], l_r.at[1, s - 1], at_zlo(s))

    def li_zhi(s):
        return remote(li2.at[j], li2.at[j], l_s.at[2, s - 1], l_r.at[2, s - 1], at_zhi(s))

    def lo_k():
        return remote(lo2, lo2r, l_s.at[3, 0], l_r.at[3, 0], sibling)

    def li_ag(s):
        return remote(li3.at[i], li3.at[i], l_s.at[4, s - 1], l_r.at[4, s - 1], at_x(s))

    def lo_ag(s):
        return remote(lo3.at[o], lo3.at[o], l_s.at[5, s - 1], l_r.at[5, s - 1], at_zlo(s))

    def lg_ag(s):
        return remote(lg.at[y], lg.at[y], l_s.at[6, s - 1], l_r.at[6, s - 1], at_y(s))

    for s in range(1, 4):
        li_x(s).start()
        lo_z(s).start()

    for s in range(1, 4):
        li_x(s).wait_recv()
    li2[j] = (lis[i] + lir[0]) + (lir[1] + lir[2])
    for s in range(1, 4):
        li_zhi(s).start()
    for s in range(1, 4):
        lo_z(s).wait_recv()
    lo2[...] = (lot[o] + lor[0]) + (lor[1] + lor[2])
    lo_k().start()

    for s in range(1, 4):
        ry_send(s).wait_recv()
    total = wb[y].astype(F32)
    for s in range(3):
        total = total + ry[s].astype(F32)
    ow[y] = total.astype(BF16)

    def ow_ag(s):
        return remote(ow.at[y], ow.at[y], ag_s.at[s - 1], ag_r.at[s - 1], at_y(s))

    for s in range(1, 4):
        ow_ag(s).start()

    for s in range(1, 4):
        li_zhi(s).wait_recv()
    li3[i] = (li2[0] + li2[1]) + (li2[2] + li2[3])
    for s in range(1, 4):
        li_ag(s).start()
    lo_k().wait_recv()
    lo3[o] = lo2[...] + lo2r[...]
    for s in range(1, 4):
        lo_ag(s).start()
    for s in range(1, 4):
        li_ag(s).wait_recv()
        lo_ag(s).wait_recv()
    lg[y, :RANK] = li3[...].reshape(RANK, width).astype(BF16)
    lg[y, RANK:] = lo3[...].reshape(RANK, width).astype(BF16)
    for s in range(1, 4):
        lg_ag(s).start()

    for s in range(1, 4):
        rz_send(s).wait_recv()
    total = sz[j].astype(F32)
    for s in range(3):
        total = total + rz[s].astype(F32)
    giv[...] = total.astype(BF16)
    gi_store = pltpu.make_async_copy(giv, gi_out, store_sem.at[0])
    gi_store.start()

    for s in range(1, 4):
        lg_ag(s).wait_recv()
    for n in range(CUSTOMERS):
        acc = jnp.zeros((2 * RANK, width), F32)
        for g in range(4):
            acc = acc + jnp.where(owner[g] == n, lg[g].astype(F32), 0.0)
        liv[n] = acc[:RANK]
        lov[n] = acc[RANK:]
    li_store = pltpu.make_async_copy(liv, li_out, store_sem.at[1])
    lo_store = pltpu.make_async_copy(lov, lo_out, store_sem.at[2])
    li_store.start()
    lo_store.start()

    for s in range(1, 4):
        ow_ag(s).wait_recv()
    gw_store = pltpu.make_async_copy(ow, gw_out, store_sem.at[3])
    gw_store.start()

    for s in range(1, 4):
        x_over_z(s).wait_send()
        g_over_z(s).wait_send()
        rz_send(s).wait_send()
        ry_send(s).wait_send()
        ow_ag(s).wait_send()
        li_x(s).wait_send()
        lo_z(s).wait_send()
        li_zhi(s).wait_send()
        li_ag(s).wait_send()
        lo_ag(s).wait_send()
        lg_ag(s).wait_send()
        for kk in range(2):
            p_send(o, kk, s).wait_send()
    for rel in range(4):
        g_to_sibling(o, rel).wait_send()
        for s in range(1, 4):
            x_over_x(j, rel, s).wait_send()
    lo_k().wait_send()
    gi_store.wait()
    li_store.wait()
    lo_store.wait()
    gw_store.wait()


def local(activations, cotangent, preact, weight, ain, aout, owner):
    tok, width = activations.shape
    blk = cotangent.shape[0]
    quarter = width // 4
    any_ = pl.BlockSpec(memory_space=pltpu.HBM)
    dma = pltpu.SemaphoreType.DMA
    v = pltpu.VMEM
    r8 = RANK // 4
    scratch = [
        v((8, blk, width), BF16),
        v((16, tok, width), BF16),
        v((blk, width), BF16),
        v((blk, width), BF16),
        v((width, width), BF16),
        v((CUSTOMERS, RANK, width), BF16),
        v((CUSTOMERS, RANK, width), BF16),
        v((RANK, width), BF16),
        v((RANK, width), BF16),
        v((width, width), BF16),
        v((8, blk, width), BF16),
        v((4, 2 * blk, width), BF16),
        v((4, tok, width), BF16),
        v((3, tok, width), BF16),
        v((tok, width), BF16),
        v((4, quarter, width), BF16),
        v((3, quarter, width), BF16),
        v((4, quarter, width), BF16),
        v((4, r8, width), F32),
        v((3, r8, width), F32),
        v((4, r8, width), F32),
        v((3, r8, width), F32),
        v((4, r8, width), F32),
        v((4, r8, width), F32),
        v((r8, width), F32),
        v((r8, width), F32),
        v((4, r8, width), F32),
        v((4, r8, width), F32),
        v((4, 2 * RANK, width), BF16),
        v((CUSTOMERS, RANK, width), F32),
        v((CUSTOMERS, RANK, width), F32),
        dma((6,)), dma((4,)),
        dma((3,)), dma((3,)), dma((4, 3)), dma((4, 3)),
        dma((3,)), dma((3,)), dma((4,)), dma((4,)),
        dma((4, 2)), dma((4, 2)), dma((3,)), dma((3,)),
        dma((3,)), dma((3,)), dma((3,)), dma((3,)),
        dma((7, 3)), dma((7, 3)),
    ]
    gi, gw, li, lo = pl.pallas_call(
        kernel,
        out_shape=(
            jax.ShapeDtypeStruct((tok, width), BF16),
            jax.ShapeDtypeStruct((4, quarter, width), BF16),
            jax.ShapeDtypeStruct((CUSTOMERS, RANK, width), F32),
            jax.ShapeDtypeStruct((CUSTOMERS, RANK, width), F32),
        ),
        in_specs=[any_] * 6 + [pl.BlockSpec(memory_space=pltpu.SMEM)],
        out_specs=[any_] * 4,
        scratch_shapes=scratch,
        compiler_params=pltpu.CompilerParams(
            collective_id=0, has_side_effects=True, vmem_limit_bytes=48 << 20
        ),
        name="mlp_backward",
    )(activations, cotangent, preact, weight, ain, aout, owner)
    return gi, gw.reshape(width, width), li, lo


def solution(mesh):
    placed = (
        P(("dp", "row"), "col"),
        P(("dp", "col"), "row"),
        P(("dp", "col"), "row"),
        P("col", "row"),
        P(None, None, "col"),
        P(None, None, "row"),
        P(),
    )
    return jax.shard_map(
        local,
        mesh=mesh,
        in_specs=placed,
        out_specs=(
            P(("dp", "row"), "col"),
            P("col", "row"),
            P(None, None, "col"),
            P(None, None, "row"),
        ),
        check_vma=False,
    )
```

```python
import functools

import jax
import jax.numpy as jnp
from jax import lax
from jax.experimental import pallas as pl
from jax.experimental.pallas import tpu as pltpu
from jax.sharding import PartitionSpec as P

MESH = pl.DeviceIdType.MESH
F32, BF16 = jnp.float32, jnp.bfloat16
SCALE = 2.0
CUSTOMERS = 3
RANK = 32
LANES = 128


def gelu_slope(v):
    return 0.5 * (1.0 + lax.erf(v * 0.7071067811865476)) + v * jnp.exp(
        -0.5 * v * v
    ) * 0.3989422804014327


def kernel(
    x_in, cot_in, pre_in, w_in, ain_in, aout_in, owner,
    gi_out, gw_out, li_out, lo_out,
    gb, xb, cotv, prev, wv, av, bv, asel, bsel, weff, pb, ra, pa, rx, sz, rza, sza, rzf, giv,
    wb, ry, ow, lgx, lgz, lgt, las, laz, lat, lg, liv, lov,
    load_sem, store_sem, xz_s, xz_r, xx_s, xx_r, g_s, g_r, gk_s, gk_r, ra_s, ra_r, rx_s, rx_r,
    rza_s, rza_r, rzf_s, rzf_r, ry_s, ry_r, ag_s, ag_r, l_s, l_r,
):
    y, r, c = lax.axis_index("dp"), lax.axis_index("row"), lax.axis_index("col")
    i, j, o, k = r // 4, r % 4, c // 2, c % 2
    sign = 1 - 2 * k
    tok = xb.shape[2]
    blk = gb.shape[1]
    width = gb.shape[2]
    wide = width // 2

    def wrap(v):
        return (v + 8) % 4

    def at_x(s):
        return (y, wrap(i + s) * 4 + j, c)

    def at_zhi(s):
        return (y, i * 4 + wrap(j + s), c)

    def at_zlo(s):
        return (y, r, wrap(o + s) * 2 + k)

    def at_y(s):
        return (wrap(y + s), r, c)

    sibling = (y, r, o * 2 + 1 - k)
    ways = (sign, -sign)

    def remote(src, dst, ss, rs, dev):
        return pltpu.make_async_remote_copy(
            src_ref=src, dst_ref=dst, send_sem=ss, recv_sem=rs, device_id=dev, device_id_type=MESH
        )

    halves = [pl.ds(0, wide), pl.ds(wide, wide)]
    loads = [
        pltpu.make_async_copy(a, b, load_sem.at[n])
        for n, (a, b) in enumerate(
            [
                (cot_in, cotv), (pre_in, prev), (w_in, wv), (ain_in, av), (aout_in, bv),
                (x_in.at[:, halves[0]], xb.at[0, r]), (x_in.at[:, halves[1]], xb.at[1, r]),
            ]
        )
    ]
    for cp in loads:
        cp.start()
    barrier = pltpu.get_barrier_semaphore()
    for s in range(1, 4):
        for dev in (at_x(s), at_zhi(s), at_zlo(s), at_y(s)):
            pl.semaphore_signal(barrier, inc=1, device_id=dev, device_id_type=MESH)
    pl.semaphore_signal(barrier, inc=1, device_id=sibling, device_id_type=MESH)

    loads[0].wait()
    loads[1].wait()
    half = blk // 2
    for h in range(2):
        rows = pl.ds(h * half, half)
        v = prev[rows, :].astype(F32)
        gb[c, rows, :] = (cotv[rows, :].astype(F32) * gelu_slope(v)).astype(BF16)
    loads[3].wait()
    loads[4].wait()
    mine = owner[y]
    a_sum = jnp.zeros(asel.shape, F32)
    b_sum = jnp.zeros(bsel.shape, F32)
    for n in range(CUSTOMERS):
        a_sum = a_sum + jnp.where(mine == n, av[n].astype(F32), 0.0)
        b_sum = b_sum + jnp.where(mine == n, bv[n].astype(F32), 0.0)
    asel[...] = a_sum.astype(BF16)
    bsel[...] = b_sum.astype(BF16)
    loads[2].wait()
    fold = lax.dot_general(asel[...], bsel[...], (((0,), (0,)), ((), ())), preferred_element_type=F32)
    weff[...] = (wv[...].astype(F32) + SCALE * fold).astype(BF16)

    def nt(a, b):
        return lax.dot_general(a, b, (((1,), (1,)), ((), ())), preferred_element_type=F32)

    lgx[i] = jnp.zeros(lgx.shape[1:], BF16)
    for h in range(2):
        lgx[i, :, h * LANES : h * LANES + half] = nt(bsel[...], gb[c, h * half : (h + 1) * half, :]).astype(BF16)
    loads[5].wait()
    loads[6].wait()
    las[k] = jnp.zeros(las.shape[1:], BF16)
    las[k, :, :tok] = (nt(asel[:, :wide], xb[0, r]) + nt(asel[:, wide:], xb[1, r])).astype(BF16)

    def lgx_send(s):
        return remote(lgx.at[i], lgx.at[i], l_s.at[0, s - 1], l_r.at[0, s - 1], at_x(s))

    def las_send():
        return remote(las.at[k], las.at[k], l_s.at[1, 0], l_r.at[1, 0], sibling)

    def lgz_send(s):
        return remote(lgz.at[j], lgz.at[j], l_s.at[2, s - 1], l_r.at[2, s - 1], at_zhi(s))

    def laz_send(s):
        return remote(laz.at[o], laz.at[o], l_s.at[3, s - 1], l_r.at[3, s - 1], at_zlo(s))

    def lgt_send(s):
        return remote(lgt.at[k, o], lgt.at[k, o], l_s.at[4, s - 1], l_r.at[4, s - 1], at_zlo(s))

    def lat_send(s):
        return remote(lat.at[i, j], lat.at[i, j], l_s.at[5, s - 1], l_r.at[5, s - 1], at_zhi(s))

    def lgt_sib():
        return remote(lgt.at[k], lgt.at[k], l_s.at[6, 0], l_r.at[6, 0], sibling)

    def lat_x(s):
        return remote(lat.at[i], lat.at[i], l_s.at[7, s - 1], l_r.at[7, s - 1], at_x(s))

    def lg_y(s):
        return remote(lg.at[y], lg.at[y], l_s.at[8, s - 1], l_r.at[8, s - 1], at_y(s))

    def xz_own(h, e):
        return remote(xb.at[h, r], xb.at[h, r], xz_s.at[h, e], xz_r.at[h, e], at_zhi(ways[e]))

    def xz_on(h):
        row = i * 4 + wrap(j - ways[h])
        return remote(xb.at[h, row], xb.at[h, row], xz_s.at[h, 2], xz_r.at[h, 2], at_zhi(ways[h]))

    def xrow(ii, q):
        return wrap(ii) * 4 + wrap(j + (0, -sign, sign, 2)[q])

    def xx_own(q, h, e):
        row = xrow(i, q)
        return remote(xb.at[h, row], xb.at[h, row], xx_s.at[q, h, e], xx_r.at[q, h, e], at_x(ways[e]))

    def xx_on(q, h):
        row = xrow(i - ways[h], q)
        return remote(xb.at[h, row], xb.at[h, row], xx_s.at[q, h, 2], xx_r.at[q, h, 2], at_x(ways[h]))

    def xx_start(q, h):
        for e in range(2):
            xx_own(q, h, e).start()

    def xx_forward(q, h):
        xx_own(q, h, h).wait_recv()
        xx_on(q, h).start()

    def g_hop(d, s):
        oo = wrap(o - s) if d == 0 else wrap(o + s)
        b = oo * 2 + k
        return remote(gb.at[b], gb.at[b], g_s.at[d, s], g_r.at[d, s], at_zlo(1 - 2 * d))

    def g_sib(d, s):
        oo = wrap(o - s) if d == 0 else wrap(o + s)
        b = oo * 2 + k
        return remote(gb.at[b], gb.at[b], gk_s.at[d, s], gk_r.at[d, s], sibling)

    def ra_send(kk):
        return remote(
            pb.at[wrap(i + 2) * 2 + kk], ra.at[kk], ra_s.at[kk], ra_r.at[kk], at_x(sign * (1 - 2 * kk))
        )

    def rx_send(kk):
        way = sign * (2 * kk - 1)
        return remote(
            pb.at[wrap(i + way) * 2 + kk], rx.at[1 - kk, kk], rx_s.at[1 - kk, kk], rx_r.at[1 - kk, kk], at_x(way)
        )

    def pa_send(kk):
        return remote(pa.at[kk], rx.at[kk, kk], rx_s.at[kk, kk], rx_r.at[kk, kk], at_x(ways[kk]))

    def part(oo, kk):
        b = oo * 2 + kk
        pb[b] = nt(gb[b], weff[...]).astype(BF16)

    def part_send(oo, kk):
        rel = wrap((oo - i) * sign)

        @pl.when(rel == 2)
        def _():
            ra_send(kk).start()

        @pl.when(rel == 3 - 2 * kk)
        def _():
            rx_send(kk).start()

    part(o, k)

    with jax.named_scope("entry"):
        pl.semaphore_wait(barrier, 13)

    with jax.named_scope("first sends"):
        for s in range(1, 4):
            lgx_send(s).start()
        las_send().start()

        @pl.when(o < 3)
        def _():
            g_hop(0, 0).start()

        @pl.when(o > 0)
        def _():
            g_hop(1, 0).start()

        g_sib(0, 0).start()
        part_send(o, k)
        for e in range(2):
            xz_own(0, e).start()
        for h in range(2):
            xx_start(0, h)
    with jax.named_scope("own block"):
        g_sib(0, 0).wait_recv()
        part(o, 1 - k)
        part_send(o, 1 - k)

    for s in range(1, 4):
        lgx_send(s).wait_recv()

    def sum4(ref):
        return (ref[0].astype(F32) + ref[1].astype(F32)) + (ref[2].astype(F32) + ref[3].astype(F32))

    with jax.named_scope("rank stage 2"):
        lgz[j] = sum4(lgx).astype(BF16)
        las_send().wait_recv()
        laz[o] = (las[0].astype(F32) + las[1].astype(F32)).astype(BF16)
        for s in range(1, 4):
            lgz_send(s).start()
            laz_send(s).start()
    def g_step(s):
        for d in range(2):
            here = (o >= s) if d == 0 else (o <= 3 - s)
            oo = wrap(o - s) if d == 0 else wrap(o + s)

            @pl.when(here)
            def _():
                g_hop(d, s - 1).wait_recv()

            @pl.when(jnp.logical_and(here, (o < 3) if d == 0 else (o > 0)))
            def _():
                g_hop(d, s).start()

            @pl.when(here)
            def _():
                g_sib(d, s).start()
                part(oo, k)
                part_send(oo, k)

        for d in range(2):
            here = (o >= s) if d == 0 else (o <= 3 - s)
            oo = wrap(o - s) if d == 0 else wrap(o + s)

            @pl.when(here)
            def _():
                g_sib(d, s).wait_recv()
                part(oo, 1 - k)
                part_send(oo, 1 - k)

    with jax.named_scope("gradients 1"):
        g_step(1)
    for e in range(2):
        xz_own(1, e).start()
    with jax.named_scope("act x own"):
        for h in range(2):
            xx_forward(0, h)
    with jax.named_scope("act z own 0"):
        for e in range(2):
            xz_own(0, e).wait_recv()
        xz_on(0).start()
        xx_start(1, 0)
        xx_start(2, 0)

    with jax.named_scope("gradients 2"):
        g_step(2)

    with jax.named_scope("rank stage 3"):
        for s in range(1, 4):
            lgz_send(s).wait_recv()
            laz_send(s).wait_recv()
        lgt[k, o] = sum4(lgz).astype(BF16)
        lat[i, j] = sum4(laz).astype(BF16)
        for s in range(1, 4):
            lgt_send(s).start()
            lat_send(s).start()
    with jax.named_scope("act z own 1"):
        for e in range(2):
            xz_own(1, e).wait_recv()
        xz_on(1).start()
        xx_start(1, 1)
        xx_start(2, 1)
    with jax.named_scope("act x on 0"):
        xx_forward(1, 0)
        xx_forward(2, 0)

    with jax.named_scope("gradients 3"):
        g_step(3)

    with jax.named_scope("input sums x"):
        for kk in range(2):
            ra_send(kk).wait_recv()
            b = wrap(i + ways[kk]) * 2 + kk
            pa[kk] = (pb[b].astype(F32) + ra[kk].astype(F32)).astype(BF16)
            pa_send(kk).start()
    with jax.named_scope("act z on 0"):
        xz_on(0).wait_recv()
        xx_start(3, 0)
    with jax.named_scope("act x on 1"):
        xx_forward(1, 1)
        xx_forward(2, 1)
    with jax.named_scope("act z on 1"):
        xz_on(1).wait_recv()
        xx_start(3, 1)
    with jax.named_scope("act x last"):
        xx_forward(3, 0)
        xx_forward(3, 1)

    with jax.named_scope("rank stage 4"):
        for s in range(1, 4):
            lgt_send(s).wait_recv()
            lat_send(s).wait_recv()
        lgt_sib().start()
        for s in range(1, 4):
            lat_x(s).start()
    def ry_send(h, s):
        return remote(wb.at[h, wrap(y + s)], ry.at[h, s - 1], ry_s.at[h, s - 1], ry_r.at[h, s - 1], at_y(s))

    gs = gb[...].reshape(8 * blk, width)

    def product(h):
        with jax.named_scope("product waits"):
            for q in range(4):
                xx_own(q, h, 1 - h).wait_recv()
                xx_on(q, h).wait_recv()
        term = lax.dot_general(
            xb[h].reshape(16 * tok, wide), gs, (((0,), (0,)), ((), ())), preferred_element_type=F32
        )
        wb[h] = term.astype(BF16).reshape(wb.shape[1:])
        for s in range(1, 4):
            ry_send(h, s).start()

    with jax.named_scope("product 0"):
        product(0)

    with jax.named_scope("input wait x"):
        for kk in range(2):
            pa_send(kk).wait_recv()
            rx_send(kk).wait_recv()
    for q in range(4):
        kk, rows = q // 2, pl.ds((q % 2) * tok, tok)
        total = pb[i * 2 + kk, rows, :].astype(F32)
        for e in range(2):
            total = total + rx[e, kk, rows, :].astype(F32)
        total = total.astype(BF16)
        sz[q, 0] = total[:, :wide]
        sz[q, 1] = total[:, wide:]

    def rza_send(h):
        return remote(sz.at[wrap(j + 2), h], rza.at[h], rza_s.at[h], rza_r.at[h], at_zhi(ways[h]))

    def rzf_send(h):
        way = ways[1 - h]
        return remote(
            sz.at[wrap(j + way), h], rzf.at[1 - h, h], rzf_s.at[1 - h, h], rzf_r.at[1 - h, h], at_zhi(way)
        )

    def sza_send(h):
        return remote(sza.at[h], rzf.at[h, h], rzf_s.at[h, h], rzf_r.at[h, h], at_zhi(ways[h]))

    for h in range(2):
        rza_send(h).start()
    for h in range(2):
        rzf_send(h).start()

    with jax.named_scope("product 1"):
        product(1)

    with jax.named_scope("adapters"):
        lgt_sib().wait_recv()
        for s in range(1, 4):
            lat_x(s).wait_recv()
        lout = jnp.zeros((RANK, width), F32)
        lin = [jnp.zeros((RANK, wide), F32), jnp.zeros((RANK, wide), F32)]
        for b in range(8):
            for p in range(2):
                row = 2 * b + p
                lout = lout + jnp.dot(
                    lat[row // 4, row % 4, :, :tok], gb[b, p * tok : (p + 1) * tok, :], preferred_element_type=F32
                )
                low = lgt[b % 2, b // 2, :, p * LANES : p * LANES + tok]
                for h in range(2):
                    lin[h] = lin[h] + jnp.dot(low, xb[h, row], preferred_element_type=F32)
        for h in range(2):
            lg[y, :RANK, h * wide : (h + 1) * wide] = (SCALE * lin[h]).astype(BF16)
        lg[y, RANK:] = (SCALE * lout).astype(BF16)
        for s in range(1, 4):
            lg_y(s).start()
    def ow_ag(h, s):
        return remote(ow.at[h, y], ow.at[h, y], ag_s.at[h, s - 1], ag_r.at[h, s - 1], at_y(s))

    def sum_y(h):
        for s in range(1, 4):
            ry_send(h, s).wait_recv()
        total = wb[h, y].astype(F32)
        for s in range(3):
            total = total + ry[h, s].astype(F32)
        ow[h, y] = total.astype(BF16)
        for s in range(1, 4):
            ow_ag(h, s).start()

    with jax.named_scope("y sum 0"):
        sum_y(0)
    with jax.named_scope("input sums z"):
        for h in range(2):
            rza_send(h).wait_recv()
            sza[h] = (sz[wrap(j + ways[h]), h].astype(F32) + rza[h].astype(F32)).astype(BF16)
            sza_send(h).start()
    with jax.named_scope("y sum 1"):
        sum_y(1)

    with jax.named_scope("adapters wait y"):
        for s in range(1, 4):
            lg_y(s).wait_recv()
    for n in range(CUSTOMERS):
        acc = jnp.zeros((2 * RANK, width), F32)
        for g in range(4):
            acc = acc + jnp.where(owner[g] == n, lg[g].astype(F32), 0.0)
        liv[n] = acc[:RANK]
        lov[n] = acc[RANK:]
    li_store = pltpu.make_async_copy(liv, li_out, store_sem.at[1])
    lo_store = pltpu.make_async_copy(lov, lo_out, store_sem.at[2])
    li_store.start()
    lo_store.start()
    with jax.named_scope("input wait z"):
        for h in range(2):
            rzf_send(h).wait_recv()
            sza_send(h).wait_recv()
    for h in range(2):
        total = sz[j, h].astype(F32)
        for e in range(2):
            total = total + rzf[e, h].astype(F32)
        giv[:, h * wide : (h + 1) * wide] = total.astype(BF16)
    gi_store = pltpu.make_async_copy(giv, gi_out, store_sem.at[0])
    gi_store.start()
    with jax.named_scope("y gather"):
        gw_stores = []
        for h in range(2):
            for s in range(1, 4):
                ow_ag(h, s).wait_recv()
            gw_stores.append(pltpu.make_async_copy(ow.at[h], gw_out.at[h], store_sem.at[3 + h]))
            gw_stores[h].start()
    with jax.named_scope("sent"):
        for d in range(2):
            for s in range(3):
                sent = (o >= s) if d == 0 else (o <= 3 - s)

                @pl.when(jnp.logical_and(sent, (o < 3) if d == 0 else (o > 0)))
                def _():
                    g_hop(d, s).wait_send()

                if s > 0 or d == 0:

                    @pl.when(sent)
                    def _():
                        g_sib(d, s).wait_send()

            @pl.when((o == 3) if d == 0 else (o == 0))
            def _():
                g_sib(d, 3).wait_send()

        for h in range(2):
            for e in range(2):
                xz_own(h, e).wait_send()
            xz_on(h).wait_send()
            for q in range(4):
                for e in range(2):
                    xx_own(q, h, e).wait_send()
                xx_on(q, h).wait_send()
            ra_send(h).wait_send()
            rx_send(h).wait_send()
            pa_send(h).wait_send()
            rza_send(h).wait_send()
            rzf_send(h).wait_send()
            sza_send(h).wait_send()
            for s in range(1, 4):
                ry_send(h, s).wait_send()
                ow_ag(h, s).wait_send()
        las_send().wait_send()
        lgt_sib().wait_send()
        for s in range(1, 4):
            for small in (lgx_send, lgz_send, laz_send, lgt_send, lat_send, lat_x, lg_y):
                small(s).wait_send()
    for cp in [gi_store, li_store, lo_store, *gw_stores]:
        cp.wait()


def local(activations, cotangent, preact, weight, ain, aout, owner):
    tok, width = activations.shape
    blk = cotangent.shape[0]
    wide = width // 2
    eighth = width // 8
    hbm = pl.BlockSpec(memory_space=pltpu.HBM)
    dma = pltpu.SemaphoreType.DMA
    v = pltpu.VMEM
    scratch = [
        v((8, blk, width), BF16),
        v((2, 16, tok, wide), BF16),
        v((blk, width), BF16),
        v((blk, width), BF16),
        v((width, width), BF16),
        v((CUSTOMERS, RANK, width), BF16),
        v((CUSTOMERS, RANK, width), BF16),
        v((RANK, width), BF16),
        v((RANK, width), BF16),
        v((width, width), BF16),
        v((8, blk, width), BF16),
        v((2, blk, width), BF16),
        v((2, blk, width), BF16),
        v((2, 2, blk, width), BF16),
        v((4, 2, tok, wide), BF16),
        v((2, tok, wide), BF16),
        v((2, tok, wide), BF16),
        v((2, 2, tok, wide), BF16),
        v((tok, width), BF16),
        v((2, 4, eighth, width), BF16),
        v((2, 3, eighth, width), BF16),
        v((2, 4, eighth, width), BF16),
        v((4, RANK, 2 * LANES), BF16),
        v((4, RANK, 2 * LANES), BF16),
        v((2, 4, RANK, 2 * LANES), BF16),
        v((2, RANK, LANES), BF16),
        v((4, RANK, LANES), BF16),
        v((4, 4, RANK, LANES), BF16),
        v((4, 2 * RANK, width), BF16),
        v((CUSTOMERS, RANK, width), F32),
        v((CUSTOMERS, RANK, width), F32),
        dma((7,)), dma((5,)),
        dma((2, 3)), dma((2, 3)), dma((4, 2, 3)), dma((4, 2, 3)),
        dma((2, 4)), dma((2, 4)), dma((2, 4)), dma((2, 4)),
        dma((2,)), dma((2,)), dma((2, 2)), dma((2, 2)),
        dma((2,)), dma((2,)), dma((2, 2)), dma((2, 2)),
        dma((2, 3)), dma((2, 3)), dma((2, 3)), dma((2, 3)),
        dma((9, 3)), dma((9, 3)),
    ]
    gi, gw, li, lo = pl.pallas_call(
        kernel,
        out_shape=(
            jax.ShapeDtypeStruct((tok, width), BF16),
            jax.ShapeDtypeStruct((2, 4, eighth, width), BF16),
            jax.ShapeDtypeStruct((CUSTOMERS, RANK, width), F32),
            jax.ShapeDtypeStruct((CUSTOMERS, RANK, width), F32),
        ),
        in_specs=[hbm] * 6 + [pl.BlockSpec(memory_space=pltpu.SMEM)],
        out_specs=[hbm] * 4,
        scratch_shapes=scratch,
        compiler_params=pltpu.CompilerParams(
            collective_id=0, has_side_effects=True, vmem_limit_bytes=60 << 20
        ),
        name="mlp_backward",
    )(activations, cotangent, preact, weight, ain, aout, owner)
    return gi, gw.reshape(width, width), li, lo


def solution(mesh):
    placed = (
        P(("dp", "row"), "col"),
        P(("dp", "col"), "row"),
        P(("dp", "col"), "row"),
        P("col", "row"),
        P(None, None, "col"),
        P(None, None, "row"),
        P(),
    )
    return jax.shard_map(
        local,
        mesh=mesh,
        in_specs=placed,
        out_specs=(
            P(("dp", "row"), "col"),
            P("col", "row"),
            P(None, None, "col"),
            P(None, None, "row"),
        ),
        check_vma=False,
    )
```

```python
import functools

import jax
import jax.numpy as jnp
from jax import lax
from jax.experimental import pallas as pl
from jax.experimental.pallas import tpu as pltpu
from jax.sharding import PartitionSpec as P

MESH = pl.DeviceIdType.MESH
F32, BF16 = jnp.float32, jnp.bfloat16
SCALE = 2.0
CUSTOMERS = 3
RANK = 32
LANES = 128
PARTS = 3


def gelu_slope(v):
    return 0.5 * (1.0 + lax.erf(v * 0.7071067811865476)) + v * jnp.exp(
        -0.5 * v * v
    ) * 0.3989422804014327


def kernel(
    x_in, cot_in, pre_in, w_in, ain_in, aout_in, owner,
    gi_out, gw_out, li_out, lo_out,
    gb, xb, cotv, prev, wv, av, bv, asel, bsel, weff, pb, ra, pa, rx, sz, rza, sza, rzf,
    wb, ryo, ryp, ryf, lgx, lgz, lgt, las, laz, lat, lg,
    load_sem, xz_s, xz_r, xx_s, xx_r, g_s, g_r, gk_s, gk_r, ra_s, ra_r, rx_s, rx_r,
    rza_s, rza_r, rzf_s, rzf_r, yo_s, yo_r, yd_s, yd_r, yp_s, yp_r, ag_s, ag_r, l_s, l_r,
):
    y, r, c = lax.axis_index("dp"), lax.axis_index("row"), lax.axis_index("col")
    i, j, o, k = r // 4, r % 4, c // 2, c % 2
    sign = 1 - 2 * k
    tok = xb.shape[2]
    blk = gb.shape[1]
    half = blk // 2
    width = gb.shape[2]
    wide = width // 2
    third = width // PARTS

    def wrap(v):
        return (v + 8) % 4

    def at_x(s):
        return (y, wrap(i + s) * 4 + j, c)

    def at_zhi(s):
        return (y, i * 4 + wrap(j + s), c)

    def at_zlo(s):
        return (y, r, wrap(o + s) * 2 + k)

    def at_y(s):
        return (wrap(y + s), r, c)

    sibling = (y, r, o * 2 + 1 - k)
    ways = (sign, -sign)

    def remote(src, dst, ss, rs, dev):
        return pltpu.make_async_remote_copy(
            src_ref=src, dst_ref=dst, send_sem=ss, recv_sem=rs, device_id=dev, device_id_type=MESH
        )

    loads = [
        pltpu.make_async_copy(a, b, load_sem.at[n])
        for n, (a, b) in enumerate(
            [(cot_in, cotv), (pre_in, prev), (w_in, wv), (ain_in, av), (aout_in, bv)]
            + [(x_in.at[:, pl.ds(t * third, third)], xb.at[t, r]) for t in range(PARTS)]
        )
    ]
    for cp in loads:
        cp.start()
    barrier = pltpu.get_barrier_semaphore()
    for s in range(1, 4):
        for dev in (at_x(s), at_zhi(s), at_zlo(s), at_y(s)):
            pl.semaphore_signal(barrier, inc=1, device_id=dev, device_id_type=MESH)
    pl.semaphore_signal(barrier, inc=1, device_id=sibling, device_id_type=MESH)

    def nt(a, b):
        return lax.dot_general(a, b, (((1,), (1,)), ((), ())), preferred_element_type=F32)

    def lgx_send(s):
        return remote(lgx.at[i], lgx.at[i], l_s.at[0, s - 1], l_r.at[0, s - 1], at_x(s))

    def las_send():
        return remote(las.at[k], las.at[k], l_s.at[1, 0], l_r.at[1, 0], sibling)

    def lgz_send(s):
        return remote(lgz.at[j], lgz.at[j], l_s.at[2, s - 1], l_r.at[2, s - 1], at_zhi(s))

    def laz_send(s):
        return remote(laz.at[o], laz.at[o], l_s.at[3, s - 1], l_r.at[3, s - 1], at_zlo(s))

    def lgt_send(s):
        return remote(lgt.at[k, o], lgt.at[k, o], l_s.at[4, s - 1], l_r.at[4, s - 1], at_zlo(s))

    def lat_send(s):
        return remote(lat.at[i, j], lat.at[i, j], l_s.at[5, s - 1], l_r.at[5, s - 1], at_zhi(s))

    def lgt_sib():
        return remote(lgt.at[k], lgt.at[k], l_s.at[6, 0], l_r.at[6, 0], sibling)

    def lat_x(s):
        return remote(lat.at[i], lat.at[i], l_s.at[7, s - 1], l_r.at[7, s - 1], at_x(s))

    def lg_y(n, s):
        return remote(lg.at[n, y], lg.at[n, y], l_s.at[8 + n, s - 1], l_r.at[8 + n, s - 1], at_y(s))

    def xz_own(h, e):
        return remote(xb.at[h, r], xb.at[h, r], xz_s.at[h, e], xz_r.at[h, e], at_zhi(ways[e]))

    def xz_on(h):
        way = ways[h % 2]
        row = i * 4 + wrap(j - way)
        return remote(xb.at[h, row], xb.at[h, row], xz_s.at[h, 2], xz_r.at[h, 2], at_zhi(way))

    def xrow(ii, q):
        return wrap(ii) * 4 + wrap(j + (0, -sign, sign, 2)[q])

    def xx_own(q, h, e):
        row = xrow(i, q)
        return remote(xb.at[h, row], xb.at[h, row], xx_s.at[q, h, e], xx_r.at[q, h, e], at_x(ways[e]))

    def xx_on(q, h):
        way = ways[h % 2]
        row = xrow(i - way, q)
        return remote(xb.at[h, row], xb.at[h, row], xx_s.at[q, h, 2], xx_r.at[q, h, 2], at_x(way))

    def xx_start(q, h):
        for e in range(2):
            xx_own(q, h, e).start()

    def xx_forward(q, h):
        xx_own(q, h, h % 2).wait_recv()
        xx_on(q, h).start()

    def g_block(d, s):
        return (wrap(o - s) if d == 0 else wrap(o + s)) * 2 + k

    def g_hop(d, s, h):
        ref = gb.at[g_block(d, s), pl.ds(h * half, half)]
        return remote(ref, ref, g_s.at[d, s, h], g_r.at[d, s, h], at_zlo(1 - 2 * d))

    def g_sib(d, s, h):
        ref = gb.at[g_block(d, s), pl.ds(h * half, half)]
        return remote(ref, ref, gk_s.at[d, s, h], gk_r.at[d, s, h], sibling)

    def ra_send(kk):
        return remote(
            pb.at[wrap(i + 2) * 2 + kk], ra.at[kk], ra_s.at[kk], ra_r.at[kk], at_x(sign * (1 - 2 * kk))
        )

    def rx_send(kk):
        way = sign * (2 * kk - 1)
        return remote(
            pb.at[wrap(i + way) * 2 + kk], rx.at[1 - kk, kk], rx_s.at[1 - kk, kk], rx_r.at[1 - kk, kk], at_x(way)
        )

    def pa_send(kk):
        return remote(pa.at[kk], rx.at[kk, kk], rx_s.at[kk, kk], rx_r.at[kk, kk], at_x(ways[kk]))

    def part(oo, kk):
        b = oo * 2 + kk
        pb[b] = nt(gb[b], weff[...]).astype(BF16)

    def part_send(oo, kk):
        rel = wrap((oo - i) * sign)

        @pl.when(rel == 2)
        def _():
            ra_send(kk).start()

        @pl.when(rel == 3 - 2 * kk)
        def _():
            rx_send(kk).start()

    loads[0].wait()
    loads[1].wait()
    for h in range(2):
        rows = pl.ds(h * half, half)
        v = prev[rows, :].astype(F32)
        gb[c, rows, :] = (cotv[rows, :].astype(F32) * gelu_slope(v)).astype(BF16)
    for t in range(PARTS):
        loads[5 + t].wait()
    with jax.named_scope("entry"):
        pl.semaphore_wait(barrier, 13)

    for h in range(2):

        @pl.when(o < 3)
        def _():
            g_hop(0, 0, h).start()

        @pl.when(o > 0)
        def _():
            g_hop(1, 0, h).start()

    for h in range(2):
        g_sib(0, 0, h).start()

    with jax.named_scope("fold"):
        loads[3].wait()
        loads[4].wait()
        mine = owner[y]
        a_sum = jnp.zeros(asel.shape, F32)
        b_sum = jnp.zeros(bsel.shape, F32)
        for n in range(CUSTOMERS):
            a_sum = a_sum + jnp.where(mine == n, av[n].astype(F32), 0.0)
            b_sum = b_sum + jnp.where(mine == n, bv[n].astype(F32), 0.0)
        asel[...] = a_sum.astype(BF16)
        bsel[...] = b_sum.astype(BF16)
        loads[2].wait()
        fold = lax.dot_general(
            asel[...], bsel[...], (((0,), (0,)), ((), ())), preferred_element_type=F32
        )
        weff[...] = (wv[...].astype(F32) + SCALE * fold).astype(BF16)

    with jax.named_scope("rank stage 1"):
        lgx[i] = jnp.zeros(lgx.shape[1:], BF16)
        for h in range(2):
            lgx[i, :, h * LANES : h * LANES + half] = nt(
                bsel[...], gb[c, h * half : (h + 1) * half, :]
            ).astype(BF16)
        las[k] = jnp.zeros(las.shape[1:], BF16)
        low = jnp.zeros((RANK, tok), F32)
        for t in range(PARTS):
            low = low + nt(asel[:, t * third : (t + 1) * third], xb[t, r])
        las[k, :, :tok] = low.astype(BF16)
        for s in range(1, 4):
            lgx_send(s).start()
        las_send().start()

    with jax.named_scope("own block"):
        part(o, k)
        part_send(o, k)
        for h in range(2):
            g_sib(0, 0, h).wait_recv()
        part(o, 1 - k)
        part_send(o, 1 - k)
        for t in range(PARTS):
            xx_start(0, t)

    def sum4(ref):
        return (ref[0].astype(F32) + ref[1].astype(F32)) + (ref[2].astype(F32) + ref[3].astype(F32))

    def g_step(s):
        for d in range(2):
            here = (o >= s) if d == 0 else (o <= 3 - s)
            oo = wrap(o - s) if d == 0 else wrap(o + s)
            for h in range(2):

                @pl.when(here)
                def _():
                    g_hop(d, s - 1, h).wait_recv()

                @pl.when(jnp.logical_and(here, (o < 3) if d == 0 else (o > 0)))
                def _():
                    g_hop(d, s, h).start()

                @pl.when(here)
                def _():
                    g_sib(d, s, h).start()

            @pl.when(here)
            def _():
                part(oo, k)
                part_send(oo, k)

        for d in range(2):
            here = (o >= s) if d == 0 else (o <= 3 - s)
            oo = wrap(o - s) if d == 0 else wrap(o + s)

            @pl.when(here)
            def _():
                for h in range(2):
                    g_sib(d, s, h).wait_recv()
                part(oo, 1 - k)
                part_send(oo, 1 - k)

    def pass_on(dist):
        with jax.named_scope(f"input sums x {dist}"):
            for kk in range(2):
                ii = wrap(i + ways[kk])

                @pl.when(jnp.logical_or(o - ii == dist, ii - o == dist))
                def _():
                    ra_send(kk).wait_recv()
                    pa[kk] = (pb[ii * 2 + kk].astype(F32) + ra[kk].astype(F32)).astype(BF16)
                    pa_send(kk).start()

    def act_z(t):
        with jax.named_scope(f"act z {t}"):
            for e in range(2):
                xz_own(t, e).wait_recv()
            xz_on(t).start()
            xx_start(1, t)
            xx_start(2, t)

    def act_z_last(t):
        with jax.named_scope(f"act z last {t}"):
            xz_on(t).wait_recv()
            xx_start(3, t)

    def act_x(q, t):
        with jax.named_scope(f"act x {q} {t}"):
            xx_forward(q, t)

    def xz_start(t):
        for e in range(2):
            xz_own(t, e).start()

    with jax.named_scope("gradients 1"):
        g_step(1)
    pass_on(0)
    for t in range(PARTS):
        act_x(0, t)
    with jax.named_scope("gradients 2"):
        g_step(2)
    xz_start(0)
    pass_on(1)
    with jax.named_scope("rank stage 2"):
        for s in range(1, 4):
            lgx_send(s).wait_recv()
        lgz[j] = sum4(lgx).astype(BF16)
        las_send().wait_recv()
        laz[o] = (las[0].astype(F32) + las[1].astype(F32)).astype(BF16)
        for s in range(1, 4):
            lgz_send(s).start()
            laz_send(s).start()
    with jax.named_scope("gradients 3"):
        g_step(3)
    xz_start(1)
    pass_on(2)
    act_z(0)
    with jax.named_scope("rank stage 3"):
        for s in range(1, 4):
            lgz_send(s).wait_recv()
            laz_send(s).wait_recv()
        lgt[k, o] = sum4(lgz).astype(BF16)
        lat[i, j] = sum4(laz).astype(BF16)
        for s in range(1, 4):
            lgt_send(s).start()
            lat_send(s).start()
    xz_start(2)
    act_x(1, 0)
    act_x(2, 0)
    act_z_last(0)
    act_z(1)
    pass_on(3)
    act_x(3, 0)
    act_x(1, 1)
    act_x(2, 1)
    act_z(2)
    act_z_last(1)
    with jax.named_scope("rank stage 4"):
        for s in range(1, 4):
            lgt_send(s).wait_recv()
            lat_send(s).wait_recv()
        lgt_sib().start()
        for s in range(1, 4):
            lat_x(s).start()
    low_rows = wb.shape[2] // 2
    cuts = (pl.ds(0, low_rows), pl.ds(low_rows, low_rows))

    def yo_send(t, e):
        return remote(
            wb.at[t, wrap(y + 2), cuts[e]], ryo.at[t, e], yo_s.at[t, e], yo_r.at[t, e], at_y(ways[e])
        )

    def yd_send(t, e):
        return remote(
            wb.at[t, wrap(y + ways[e]), cuts[1 - e]], ryf.at[t, e, 1 - e], yd_s.at[t, e], yd_r.at[t, e], at_y(ways[e])
        )

    def yp_send(t, e):
        return remote(ryp.at[t, e], ryf.at[t, e, e], yp_s.at[t, e], yp_r.at[t, e], at_y(ways[e]))

    def pass_y(t):
        with jax.named_scope(f"y pass {t}"):
            for e in range(2):
                yo_send(t, e).wait_recv()
                own = wb[t, wrap(y + ways[e]), cuts[e], :].astype(F32)
                ryp[t, e] = (own + ryo[t, e].astype(F32)).astype(BF16)
                yp_send(t, e).start()

    gs = gb[...].reshape(8 * blk, width)

    def product(t):
        with jax.named_scope(f"product waits {t}"):
            for q in range(4):
                xx_own(q, t, 1 - t % 2).wait_recv()
                xx_on(q, t).wait_recv()
        with jax.named_scope(f"product {t}"):
            term = lax.dot_general(
                xb[t].reshape(16 * tok, third), gs, (((0,), (0,)), ((), ())), preferred_element_type=F32
            )
            wb[t] = term.astype(BF16).reshape(wb.shape[1:])
            for e in range(2):
                yo_send(t, e).start()
            for e in range(2):
                yd_send(t, e).start()

    def rza_send(h):
        return remote(sz.at[wrap(j + 2), h], rza.at[h], rza_s.at[h], rza_r.at[h], at_zhi(ways[h]))

    def rzf_send(h):
        way = ways[1 - h]
        return remote(
            sz.at[wrap(j + way), h], rzf.at[1 - h, h], rzf_s.at[1 - h, h], rzf_r.at[1 - h, h], at_zhi(way)
        )

    def sza_send(h):
        return remote(sza.at[h], rzf.at[h, h], rzf_s.at[h, h], rzf_r.at[h, h], at_zhi(ways[h]))

    def input_x():
        with jax.named_scope("input wait x"):
            for kk in range(2):
                pa_send(kk).wait_recv()
                rx_send(kk).wait_recv()
        for q in range(4):
            kk, rows = q // 2, pl.ds((q % 2) * tok, tok)
            total = pb[i * 2 + kk, rows, :].astype(F32)
            for e in range(2):
                total = total + rx[e, kk, rows, :].astype(F32)
            total = total.astype(BF16)
            sz[q, 0] = total[:, :wide]
            sz[q, 1] = total[:, wide:]
        for h in range(2):
            rza_send(h).start()
        for h in range(2):
            rzf_send(h).start()

    def lo_part():
        with jax.named_scope("adapter out"):
            for s in range(1, 4):
                lat_x(s).wait_recv()
            lout = jnp.zeros((RANK, width), F32)
            for row in range(16):
                b, p = row // 2, row % 2
                lout = lout + jnp.dot(
                    lat[row // 4, row % 4, :, :tok],
                    gb[b, p * tok : (p + 1) * tok, :],
                    preferred_element_type=F32,
                )
            lg[1, y] = (SCALE * lout).astype(BF16)
            for s in range(1, 4):
                lg_y(1, s).start()

    def li_part(t):
        with jax.named_scope(f"adapter in {t}"):
            if t == 0:
                lgt_sib().wait_recv()
            lin = jnp.zeros((RANK, third), F32)
            for row in range(16):
                b, p = row // 2, row % 2
                low = lgt[b % 2, b // 2, :, p * LANES : p * LANES + tok]
                lin = lin + jnp.dot(low, xb[t, row], preferred_element_type=F32)
            lg[0, y, :, t * third : (t + 1) * third] = (SCALE * lin).astype(BF16)
            if t == PARTS - 1:
                for s in range(1, 4):
                    lg_y(0, s).start()

    def ag_own(t, e):
        return remote(gw_out.at[t, y], gw_out.at[t, y], ag_s.at[t, e], ag_r.at[t, e], at_y(ways[e]))

    def ag_on(t, e):
        ref = gw_out.at[t, wrap(y - ways[e]), cuts[e]]
        return remote(ref, ref, ag_s.at[t, 2 + e], ag_r.at[t, 2 + e], at_y(ways[e]))

    def sum_y(t):
        with jax.named_scope(f"y sum {t}"):
            for e in range(2):
                yd_send(t, e).wait_recv()
                yp_send(t, e).wait_recv()
            for h in range(2):
                total = wb[t, y, cuts[h], :].astype(F32)
                for e in range(2):
                    total = total + ryf[t, e, h].astype(F32)
                gw_out[t, y, cuts[h], :] = total.astype(BF16)
            for e in range(2):
                ag_own(t, e).start()

    def spread_y(t):
        with jax.named_scope(f"y spread {t}"):
            for e in range(2):
                ag_own(t, e).wait_recv()
                ag_on(t, e).start()

    def pass_z():
        with jax.named_scope("input sums z"):
            for h in range(2):
                rza_send(h).wait_recv()
                sza[h] = (sz[wrap(j + ways[h]), h].astype(F32) + rza[h].astype(F32)).astype(BF16)
                sza_send(h).start()

    product(0)
    act_x(1, 2)
    act_x(2, 2)
    act_z_last(2)
    input_x()
    act_x(3, 1)
    pass_y(0)
    product(1)
    act_x(3, 2)
    sum_y(0)
    product(2)
    pass_y(1)
    pass_z()
    lo_part()
    for t in range(PARTS):
        li_part(t)
    spread_y(0)
    sum_y(1)
    pass_y(2)
    spread_y(1)
    sum_y(2)

    with jax.named_scope("input wait z"):
        for h in range(2):
            rzf_send(h).wait_recv()
            sza_send(h).wait_recv()
    for h in range(2):
        total = sz[j, h].astype(F32)
        for e in range(2):
            total = total + rzf[e, h].astype(F32)
        gi_out[:, h * wide : (h + 1) * wide] = total.astype(BF16)
    with jax.named_scope("adapters wait y"):
        for s in range(1, 4):
            for n in range(2):
                lg_y(n, s).wait_recv()
    for n in range(CUSTOMERS):
        for m, ref in enumerate((li_out, lo_out)):
            acc = jnp.zeros((RANK, width), F32)
            for g in range(4):
                acc = acc + jnp.where(owner[g] == n, lg[m, g].astype(F32), 0.0)
            ref[n] = acc
    spread_y(2)
    with jax.named_scope("y gather"):
        for t in range(PARTS):
            for e in range(2):
                ag_on(t, e).wait_recv()

    with jax.named_scope("sent"):
        for d in range(2):
            for s in range(4):
                sent = (o >= s) if d == 0 else (o <= 3 - s)
                if s < 3:

                    @pl.when(jnp.logical_and(sent, (o < 3) if d == 0 else (o > 0)))
                    def _():
                        for h in range(2):
                            g_hop(d, s, h).wait_send()

                if s > 0 or d == 0:

                    @pl.when(sent)
                    def _():
                        for h in range(2):
                            g_sib(d, s, h).wait_send()

        for t in range(PARTS):
            for e in range(2):
                xz_own(t, e).wait_send()
            xz_on(t).wait_send()
            for q in range(4):
                for e in range(2):
                    xx_own(q, t, e).wait_send()
                xx_on(q, t).wait_send()
            for e in range(2):
                yo_send(t, e).wait_send()
                yd_send(t, e).wait_send()
                yp_send(t, e).wait_send()
                ag_own(t, e).wait_send()
                ag_on(t, e).wait_send()
        for h in range(2):
            ra_send(h).wait_send()
            rx_send(h).wait_send()
            pa_send(h).wait_send()
            rza_send(h).wait_send()
            rzf_send(h).wait_send()
            sza_send(h).wait_send()
        las_send().wait_send()
        lgt_sib().wait_send()
        for s in range(1, 4):
            for small in (lgx_send, lgz_send, laz_send, lgt_send, lat_send, lat_x):
                small(s).wait_send()
            for n in range(2):
                lg_y(n, s).wait_send()


def local(activations, cotangent, preact, weight, ain, aout, owner):
    tok, width = activations.shape
    blk = cotangent.shape[0]
    wide = width // 2
    third = width // PARTS
    piece = third // 4
    hbm = pl.BlockSpec(memory_space=pltpu.HBM)
    dma = pltpu.SemaphoreType.DMA
    v = pltpu.VMEM
    scratch = [
        v((8, blk, width), BF16),
        v((PARTS, 16, tok, third), BF16),
        v((blk, width), BF16),
        v((blk, width), BF16),
        v((width, width), BF16),
        v((CUSTOMERS, RANK, width), BF16),
        v((CUSTOMERS, RANK, width), BF16),
        v((RANK, width), BF16),
        v((RANK, width), BF16),
        v((width, width), BF16),
        v((8, blk, width), BF16),
        v((2, blk, width), BF16),
        v((2, blk, width), BF16),
        v((2, 2, blk, width), BF16),
        v((4, 2, tok, wide), BF16),
        v((2, tok, wide), BF16),
        v((2, tok, wide), BF16),
        v((2, 2, tok, wide), BF16),
        v((PARTS, 4, piece, width), BF16),
        v((PARTS, 2, piece // 2, width), BF16),
        v((PARTS, 2, piece // 2, width), BF16),
        v((PARTS, 2, 2, piece // 2, width), BF16),
        v((4, RANK, 2 * LANES), BF16),
        v((4, RANK, 2 * LANES), BF16),
        v((2, 4, RANK, 2 * LANES), BF16),
        v((2, RANK, LANES), BF16),
        v((4, RANK, LANES), BF16),
        v((4, 4, RANK, LANES), BF16),
        v((2, 4, RANK, width), BF16),
        dma((8,)),
        dma((PARTS, 3)), dma((PARTS, 3)), dma((4, PARTS, 3)), dma((4, PARTS, 3)),
        dma((2, 4, 2)), dma((2, 4, 2)), dma((2, 4, 2)), dma((2, 4, 2)),
        dma((2,)), dma((2,)), dma((2, 2)), dma((2, 2)),
        dma((2,)), dma((2,)), dma((2, 2)), dma((2, 2)),
        dma((PARTS, 2)), dma((PARTS, 2)), dma((PARTS, 2)), dma((PARTS, 2)),
        dma((PARTS, 2)), dma((PARTS, 2)), dma((PARTS, 4)), dma((PARTS, 4)),
        dma((10, 3)), dma((10, 3)),
    ]
    gi, gw, li, lo = pl.pallas_call(
        kernel,
        out_shape=(
            pltpu.VMEM((tok, width), BF16),
            pltpu.VMEM((PARTS, 4, piece, width), BF16),
            pltpu.VMEM((CUSTOMERS, RANK, width), F32),
            pltpu.VMEM((CUSTOMERS, RANK, width), F32),
        ),
        in_specs=[hbm] * 6 + [pl.BlockSpec(memory_space=pltpu.SMEM)],
        out_specs=[pl.BlockSpec(memory_space=pltpu.VMEM)] * 4,
        scratch_shapes=scratch,
        compiler_params=pltpu.CompilerParams(
            collective_id=0, has_side_effects=True, vmem_limit_bytes=60 << 20
        ),
        name="mlp_backward",
    )(activations, cotangent, preact, weight, ain, aout, owner)
    return gi, gw.reshape(width, width), li, lo


def solution(mesh):
    placed = (
        P(("dp", "row"), "col"),
        P(("dp", "col"), "row"),
        P(("dp", "col"), "row"),
        P("col", "row"),
        P(None, None, "col"),
        P(None, None, "row"),
        P(),
    )
    return jax.shard_map(
        local,
        mesh=mesh,
        in_specs=placed,
        out_specs=(
            P(("dp", "row"), "col"),
            P("col", "row"),
            P(None, None, "col"),
            P(None, None, "row"),
        ),
        check_vma=False,
    )
```

```python
import functools

import jax
import jax.numpy as jnp
from jax import lax
from jax.experimental import pallas as pl
from jax.experimental.pallas import tpu as pltpu
from jax.sharding import PartitionSpec as P

MESH = pl.DeviceIdType.MESH
F32, BF16 = jnp.float32, jnp.bfloat16
SCALE = 2.0
CUSTOMERS = 3
RANK = 32
LANES = 128
PARTS = 3
DIRECT = 3


def gelu_slope(v):
    return 0.5 * (1.0 + lax.erf(v * 0.7071067811865476)) + v * jnp.exp(
        -0.5 * v * v
    ) * 0.3989422804014327


def kernel(
    x_in, cot_in, pre_in, w_in, ain_in, aout_in, owner,
    gi_out, gw_out, li_out, lo_out,
    gb, xb, cotv, prev, wv, av, bv, asel, bsel, weff, pb, ra, pa, rx, sz, rza, sza, rzf,
    wb, ryo, ryp, ryf, lgx, lgz, lgt, las, laz, lat, lg,
    load_sem, xz_s, xz_r, xx_s, xx_r, g_s, g_r, gk_s, gk_r, ra_s, ra_r, rx_s, rx_r,
    rza_s, rza_r, rzf_s, rzf_r, yo_s, yo_r, yd_s, yd_r, yp_s, yp_r, ag_s, ag_r, l_s, l_r,
):
    y, r, c = lax.axis_index("dp"), lax.axis_index("row"), lax.axis_index("col")
    i, j, o, k = r // 4, r % 4, c // 2, c % 2
    sign = 1 - 2 * k
    tok = xb.shape[2]
    blk = gb.shape[1]
    half = blk // 2
    width = gb.shape[2]
    wide = width // 2
    third = width // PARTS

    def wrap(v):
        return (v + 8) % 4

    def at_x(s):
        return (y, wrap(i + s) * 4 + j, c)

    def at_zhi(s):
        return (y, i * 4 + wrap(j + s), c)

    def at_zlo(s):
        return (y, r, wrap(o + s) * 2 + k)

    def at_y(s):
        return (wrap(y + s), r, c)

    sibling = (y, r, o * 2 + 1 - k)
    ways = (sign, -sign)

    def remote(src, dst, ss, rs, dev):
        return pltpu.make_async_remote_copy(
            src_ref=src, dst_ref=dst, send_sem=ss, recv_sem=rs, device_id=dev, device_id_type=MESH
        )

    loads = [
        pltpu.make_async_copy(a, b, load_sem.at[n])
        for n, (a, b) in enumerate(
            [(cot_in, cotv), (pre_in, prev), (w_in, wv), (ain_in, av), (aout_in, bv)]
            + [(x_in.at[:, pl.ds(t * third, third)], xb.at[t, r]) for t in range(PARTS)]
        )
    ]
    early = [loads[0], loads[1], *loads[5:]]
    late = loads[2:5]
    for cp in early:
        cp.start()
    barrier = pltpu.get_barrier_semaphore()
    for s in range(1, 4):
        for dev in (at_x(s), at_zhi(s), at_zlo(s), at_y(s)):
            pl.semaphore_signal(barrier, inc=1, device_id=dev, device_id_type=MESH)
    pl.semaphore_signal(barrier, inc=1, device_id=sibling, device_id_type=MESH)

    def nt(a, b):
        return lax.dot_general(a, b, (((1,), (1,)), ((), ())), preferred_element_type=F32)

    def lgx_send(s):
        return remote(lgx.at[i], lgx.at[i], l_s.at[0, s - 1], l_r.at[0, s - 1], at_x(s))

    def las_send():
        return remote(las.at[k], las.at[k], l_s.at[1, 0], l_r.at[1, 0], sibling)

    def lgz_send(s):
        return remote(lgz.at[j], lgz.at[j], l_s.at[2, s - 1], l_r.at[2, s - 1], at_zhi(s))

    def laz_send(s):
        return remote(laz.at[o], laz.at[o], l_s.at[3, s - 1], l_r.at[3, s - 1], at_zlo(s))

    def lgt_send(s):
        return remote(lgt.at[k, o], lgt.at[k, o], l_s.at[4, s - 1], l_r.at[4, s - 1], at_zlo(s))

    def lat_send(s):
        return remote(lat.at[i, j], lat.at[i, j], l_s.at[5, s - 1], l_r.at[5, s - 1], at_zhi(s))

    def lgt_sib():
        return remote(lgt.at[k], lgt.at[k], l_s.at[6, 0], l_r.at[6, 0], sibling)

    def lat_x(s):
        return remote(lat.at[i], lat.at[i], l_s.at[7, s - 1], l_r.at[7, s - 1], at_x(s))

    def lg_y(n, s):
        return remote(lg.at[n, y], lg.at[n, y], l_s.at[8 + n, s - 1], l_r.at[8 + n, s - 1], at_y(s))

    def xz_own(h, e):
        return remote(xb.at[h, r], xb.at[h, r], xz_s.at[h, e], xz_r.at[h, e], at_zhi(ways[e]))

    def xz_on(h):
        way = ways[h % 2]
        row = i * 4 + wrap(j - way)
        return remote(xb.at[h, row], xb.at[h, row], xz_s.at[h, 2], xz_r.at[h, 2], at_zhi(way))

    def xrow(ii, q):
        return wrap(ii) * 4 + wrap(j + (0, -sign, sign, 2)[q])

    def xx_own(q, h, e):
        row = xrow(i, q)
        return remote(xb.at[h, row], xb.at[h, row], xx_s.at[q, h, e], xx_r.at[q, h, e], at_x(ways[e]))

    def xx_on(q, h):
        way = ways[h % 2]
        row = xrow(i - way, q)
        return remote(xb.at[h, row], xb.at[h, row], xx_s.at[q, h, 2], xx_r.at[q, h, 2], at_x(way))

    def xx_direct(q, h):
        row = xrow(i, q)
        return remote(xb.at[h, row], xb.at[h, row], xx_s.at[q, h, 2], xx_r.at[q, h, 2], at_x(2))

    def xx_start(q, h):
        for e in range(2):
            xx_own(q, h, e).start()
        if q == DIRECT:
            xx_direct(q, h).start()

    def xx_forward(q, h):
        xx_own(q, h, h % 2).wait_recv()
        xx_on(q, h).start()

    def g_block(d, s):
        return (wrap(o - s) if d == 0 else wrap(o + s)) * 2 + k

    def g_hop(d, s, h):
        ref = gb.at[g_block(d, s), pl.ds(h * half, half)]
        return remote(ref, ref, g_s.at[d, s, h], g_r.at[d, s, h], at_zlo(1 - 2 * d))

    def g_sib(d, s, h):
        ref = gb.at[g_block(d, s), pl.ds(h * half, half)]
        return remote(ref, ref, gk_s.at[d, s, h], gk_r.at[d, s, h], sibling)

    def ra_send(kk):
        return remote(
            pb.at[wrap(i + 2) * 2 + kk], ra.at[kk], ra_s.at[kk], ra_r.at[kk], at_x(sign * (1 - 2 * kk))
        )

    def rx_send(kk):
        way = sign * (2 * kk - 1)
        return remote(
            pb.at[wrap(i + way) * 2 + kk], rx.at[1 - kk, kk], rx_s.at[1 - kk, kk], rx_r.at[1 - kk, kk], at_x(way)
        )

    def pa_send(kk):
        return remote(pa.at[kk], rx.at[kk, kk], rx_s.at[kk, kk], rx_r.at[kk, kk], at_x(ways[kk]))

    def part(oo, kk):
        b = oo * 2 + kk
        pb[b] = nt(gb[b], weff[...]).astype(BF16)

    def part_send(oo, kk):
        rel = wrap((oo - i) * sign)

        @pl.when(rel == 2)
        def _():
            ra_send(kk).start()

        @pl.when(rel == 3 - 2 * kk)
        def _():
            rx_send(kk).start()

    loads[0].wait()
    loads[1].wait()
    for cp in late:
        cp.start()
    for h in range(2):
        rows = pl.ds(h * half, half)
        v = prev[rows, :].astype(F32)
        gb[c, rows, :] = (cotv[rows, :].astype(F32) * gelu_slope(v)).astype(BF16)
    for t in range(PARTS):
        loads[5 + t].wait()
    with jax.named_scope("entry"):
        pl.semaphore_wait(barrier, 13)

    for h in range(2):

        @pl.when(o < 3)
        def _():
            g_hop(0, 0, h).start()

        @pl.when(o > 0)
        def _():
            g_hop(1, 0, h).start()

    for h in range(2):
        g_sib(0, 0, h).start()

    with jax.named_scope("fold"):
        loads[3].wait()
        loads[4].wait()
        mine = owner[y]
        a_sum = jnp.zeros(asel.shape, F32)
        b_sum = jnp.zeros(bsel.shape, F32)
        for n in range(CUSTOMERS):
            a_sum = a_sum + jnp.where(mine == n, av[n].astype(F32), 0.0)
            b_sum = b_sum + jnp.where(mine == n, bv[n].astype(F32), 0.0)
        asel[...] = a_sum.astype(BF16)
        bsel[...] = b_sum.astype(BF16)
        loads[2].wait()
        fold = lax.dot_general(
            asel[...], bsel[...], (((0,), (0,)), ((), ())), preferred_element_type=F32
        )
        weff[...] = (wv[...].astype(F32) + SCALE * fold).astype(BF16)

    with jax.named_scope("rank stage 1"):
        lgx[i] = jnp.zeros(lgx.shape[1:], BF16)
        for h in range(2):
            lgx[i, :, h * LANES : h * LANES + half] = nt(
                bsel[...], gb[c, h * half : (h + 1) * half, :]
            ).astype(BF16)
        las[k] = jnp.zeros(las.shape[1:], BF16)
        low = jnp.zeros((RANK, tok), F32)
        for t in range(PARTS):
            low = low + nt(asel[:, t * third : (t + 1) * third], xb[t, r])
        las[k, :, :tok] = low.astype(BF16)
        for s in range(1, 4):
            lgx_send(s).start()
        las_send().start()

    with jax.named_scope("own block"):
        part(o, k)
        part_send(o, k)
        for h in range(2):
            g_sib(0, 0, h).wait_recv()
        part(o, 1 - k)
        part_send(o, 1 - k)
        for t in range(PARTS):
            xx_start(0, t)

    def sum4(ref):
        return (ref[0].astype(F32) + ref[1].astype(F32)) + (ref[2].astype(F32) + ref[3].astype(F32))

    def g_step(s):
        here = (o >= s, o <= 3 - s)
        more = (o < 3, o > 0)
        for h in range(2):
            for d in range(2):

                @pl.when(here[d])
                def _():
                    g_hop(d, s - 1, h).wait_recv()

                @pl.when(jnp.logical_and(here[d], more[d]))
                def _():
                    g_hop(d, s, h).start()

                @pl.when(here[d])
                def _():
                    g_sib(d, s, h).start()

        for own in range(2):
            for d in range(2):
                oo = wrap(o - s) if d == 0 else wrap(o + s)

                @pl.when(here[d])
                def _():
                    kk = k if own == 0 else 1 - k
                    if own == 1:
                        for h in range(2):
                            g_sib(d, s, h).wait_recv()
                    part(oo, kk)
                    part_send(oo, kk)

    def pass_on(dist):
        with jax.named_scope(f"input sums x {dist}"):
            for kk in range(2):
                ii = wrap(i + ways[kk])

                @pl.when(jnp.logical_or(o - ii == dist, ii - o == dist))
                def _():
                    ra_send(kk).wait_recv()
                    pa[kk] = (pb[ii * 2 + kk].astype(F32) + ra[kk].astype(F32)).astype(BF16)
                    pa_send(kk).start()

    def act_z(t):
        with jax.named_scope(f"act z {t}"):
            for e in range(2):
                xz_own(t, e).wait_recv()
            xz_on(t).start()
            xx_start(1, t)
            xx_start(2, t)

    def act_z_last(t):
        with jax.named_scope(f"act z last {t}"):
            xz_on(t).wait_recv()
            xx_start(3, t)

    def act_x(q, t):
        with jax.named_scope(f"act x {q} {t}"):
            xx_forward(q, t)

    def xz_start(t):
        for e in range(2):
            xz_own(t, e).start()

    with jax.named_scope("gradients 1"):
        g_step(1)
    pass_on(0)
    for t in range(PARTS):
        act_x(0, t)
    with jax.named_scope("gradients 2"):
        g_step(2)
    pass_on(1)
    with jax.named_scope("gradients 3"):
        g_step(3)
    with jax.named_scope("gradients out"):
        for d in range(2):

            @pl.when((o == 2) if d == 0 else (o == 1))
            def _():
                for h in range(2):
                    g_hop(d, 2, h).wait_send()

    xz_start(0)
    pass_on(2)
    with jax.named_scope("rank stage 2"):
        for s in range(1, 4):
            lgx_send(s).wait_recv()
        lgz[j] = sum4(lgx).astype(BF16)
        las_send().wait_recv()
        laz[o] = (las[0].astype(F32) + las[1].astype(F32)).astype(BF16)
        for s in range(1, 4):
            lgz_send(s).start()
            laz_send(s).start()
    act_z(0)
    xz_start(1)
    pass_on(3)
    act_x(1, 0)
    act_x(2, 0)
    act_z_last(0)
    act_z(1)
    xz_start(2)
    with jax.named_scope("rank stage 3"):
        for s in range(1, 4):
            lgz_send(s).wait_recv()
            laz_send(s).wait_recv()
        lgt[k, o] = sum4(lgz).astype(BF16)
        lat[i, j] = sum4(laz).astype(BF16)
        for s in range(1, 4):
            lgt_send(s).start()
            lat_send(s).start()
    act_x(1, 1)
    act_x(2, 1)
    act_z_last(1)
    act_z(2)

    low_rows = wb.shape[2] // 2
    cuts = (pl.ds(0, low_rows), pl.ds(low_rows, low_rows))

    def yo_send(t, e):
        return remote(
            wb.at[t, wrap(y + 2), cuts[e]], ryo.at[t, e], yo_s.at[t, e], yo_r.at[t, e], at_y(ways[e])
        )

    def yd_send(t, e):
        return remote(
            wb.at[t, wrap(y + ways[e]), cuts[1 - e]], ryf.at[t, e, 1 - e], yd_s.at[t, e], yd_r.at[t, e], at_y(ways[e])
        )

    def yp_send(t, e):
        return remote(ryp.at[t, e], ryf.at[t, e, e], yp_s.at[t, e], yp_r.at[t, e], at_y(ways[e]))

    def pass_y(t):
        with jax.named_scope(f"y pass {t}"):
            for e in range(2):
                yo_send(t, e).wait_recv()
                own = wb[t, wrap(y + ways[e]), cuts[e], :].astype(F32)
                ryp[t, e] = (own + ryo[t, e].astype(F32)).astype(BF16)
                yp_send(t, e).start()

    gs = gb[...].reshape(8 * blk, width)

    def product(t):
        with jax.named_scope(f"product waits {t}"):
            for q in range(4):
                if q == DIRECT:
                    xx_own(q, t, t % 2).wait_recv()
                xx_own(q, t, 1 - t % 2).wait_recv()
                xx_on(q, t).wait_recv()
        with jax.named_scope(f"product {t}"):
            term = lax.dot_general(
                xb[t].reshape(16 * tok, third), gs, (((0,), (0,)), ((), ())), preferred_element_type=F32
            )
            wb[t] = term.astype(BF16).reshape(wb.shape[1:])
            for e in range(2):
                yo_send(t, e).start()
            for e in range(2):
                yd_send(t, e).start()

    def rza_send(h):
        return remote(sz.at[wrap(j + 2), h], rza.at[h], rza_s.at[h], rza_r.at[h], at_zhi(ways[h]))

    def rzf_send(h):
        way = ways[1 - h]
        return remote(
            sz.at[wrap(j + way), h], rzf.at[1 - h, h], rzf_s.at[1 - h, h], rzf_r.at[1 - h, h], at_zhi(way)
        )

    def sza_send(h):
        return remote(sza.at[h], rzf.at[h, h], rzf_s.at[h, h], rzf_r.at[h, h], at_zhi(ways[h]))

    def input_x():
        with jax.named_scope("input wait x"):
            for kk in range(2):
                pa_send(kk).wait_recv()
                rx_send(kk).wait_recv()
        for q in range(4):
            kk, rows = q // 2, pl.ds((q % 2) * tok, tok)
            total = pb[i * 2 + kk, rows, :].astype(F32)
            for e in range(2):
                total = total + rx[e, kk, rows, :].astype(F32)
            total = total.astype(BF16)
            sz[q, 0] = total[:, :wide]
            sz[q, 1] = total[:, wide:]
        for h in range(2):
            rza_send(h).start()

    def lo_part():
        with jax.named_scope("adapter out"):
            for s in range(1, 4):
                lat_x(s).wait_recv()
            lout = jnp.zeros((RANK, width), F32)
            for row in range(16):
                b, p = row // 2, row % 2
                lout = lout + jnp.dot(
                    lat[row // 4, row % 4, :, :tok],
                    gb[b, p * tok : (p + 1) * tok, :],
                    preferred_element_type=F32,
                )
            lg[1, y] = (SCALE * lout).astype(BF16)
            for s in range(1, 4):
                lg_y(1, s).start()

    def li_part(t):
        with jax.named_scope(f"adapter in {t}"):
            if t == 0:
                lgt_sib().wait_recv()
            lin = jnp.zeros((RANK, third), F32)
            for row in range(16):
                b, p = row // 2, row % 2
                low = lgt[b % 2, b // 2, :, p * LANES : p * LANES + tok]
                lin = lin + jnp.dot(low, xb[t, row], preferred_element_type=F32)
            lg[0, y, :, t * third : (t + 1) * third] = (SCALE * lin).astype(BF16)
            if t == PARTS - 1:
                for s in range(1, 4):
                    lg_y(0, s).start()

    def ag_own(t, e):
        return remote(gw_out.at[t, y], gw_out.at[t, y], ag_s.at[t, e], ag_r.at[t, e], at_y(ways[e]))

    def ag_on(t, e):
        ref = gw_out.at[t, wrap(y - ways[e]), cuts[e]]
        return remote(ref, ref, ag_s.at[t, 2 + e], ag_r.at[t, 2 + e], at_y(ways[e]))

    def sum_y(t):
        with jax.named_scope(f"y sum {t}"):
            for e in range(2):
                yd_send(t, e).wait_recv()
                yp_send(t, e).wait_recv()
            for h in range(2):
                total = wb[t, y, cuts[h], :].astype(F32)
                for e in range(2):
                    total = total + ryf[t, e, h].astype(F32)
                gw_out[t, y, cuts[h], :] = total.astype(BF16)
            for e in range(2):
                ag_own(t, e).start()

    def spread_y(t):
        with jax.named_scope(f"y spread {t}"):
            for e in range(2):
                ag_own(t, e).wait_recv()
                ag_on(t, e).start()

    def pass_z():
        with jax.named_scope("input sums z"):
            for h in range(2):
                rza_send(h).wait_recv()
                sza[h] = (sz[wrap(j + ways[h]), h].astype(F32) + rza[h].astype(F32)).astype(BF16)
                sza_send(h).start()
            for h in range(2):
                rzf_send(h).start()

    product(0)
    act_x(1, 2)
    act_x(2, 2)
    act_z_last(2)
    input_x()
    pass_y(0)
    product(1)
    with jax.named_scope("rank stage 4"):
        for s in range(1, 4):
            lgt_send(s).wait_recv()
            lat_send(s).wait_recv()
        lgt_sib().start()
        for s in range(1, 4):
            lat_x(s).start()
    sum_y(0)
    product(2)
    pass_y(1)
    lo_part()
    for t in range(PARTS):
        li_part(t)
    pass_y(2)
    sum_y(1)
    spread_y(0)
    pass_z()
    sum_y(2)
    spread_y(1)
    spread_y(2)

    with jax.named_scope("input wait z"):
        for h in range(2):
            rzf_send(h).wait_recv()
            sza_send(h).wait_recv()
    for h in range(2):
        total = sz[j, h].astype(F32)
        for e in range(2):
            total = total + rzf[e, h].astype(F32)
        gi_out[:, h * wide : (h + 1) * wide] = total.astype(BF16)
    with jax.named_scope("adapters wait y"):
        for s in range(1, 4):
            for n in range(2):
                lg_y(n, s).wait_recv()
    for n in range(CUSTOMERS):
        for m, ref in enumerate((li_out, lo_out)):
            acc = jnp.zeros((RANK, width), F32)
            for g in range(4):
                acc = acc + jnp.where(owner[g] == n, lg[m, g].astype(F32), 0.0)
            ref[n] = acc
    with jax.named_scope("y gather"):
        for t in range(PARTS):
            for e in range(2):
                ag_on(t, e).wait_recv()

    with jax.named_scope("sent"):
        for d in range(2):
            for s in range(4):
                sent = (o >= s) if d == 0 else (o <= 3 - s)
                if s < 2:

                    @pl.when(jnp.logical_and(sent, (o < 3) if d == 0 else (o > 0)))
                    def _():
                        for h in range(2):
                            g_hop(d, s, h).wait_send()

                if s > 0 or d == 0:

                    @pl.when(sent)
                    def _():
                        for h in range(2):
                            g_sib(d, s, h).wait_send()

        for t in range(PARTS):
            for e in range(2):
                xz_own(t, e).wait_send()
            xz_on(t).wait_send()
            for q in range(4):
                for e in range(2):
                    xx_own(q, t, e).wait_send()
                xx_on(q, t).wait_send()
            for e in range(2):
                yo_send(t, e).wait_send()
                yd_send(t, e).wait_send()
                yp_send(t, e).wait_send()
                ag_own(t, e).wait_send()
                ag_on(t, e).wait_send()
        for h in range(2):
            ra_send(h).wait_send()
            rx_send(h).wait_send()
            pa_send(h).wait_send()
            rza_send(h).wait_send()
            rzf_send(h).wait_send()
            sza_send(h).wait_send()
        las_send().wait_send()
        lgt_sib().wait_send()
        for s in range(1, 4):
            for small in (lgx_send, lgz_send, laz_send, lgt_send, lat_send, lat_x):
                small(s).wait_send()
            for n in range(2):
                lg_y(n, s).wait_send()


def local(activations, cotangent, preact, weight, ain, aout, owner):
    tok, width = activations.shape
    blk = cotangent.shape[0]
    wide = width // 2
    third = width // PARTS
    piece = third // 4
    hbm = pl.BlockSpec(memory_space=pltpu.HBM)
    dma = pltpu.SemaphoreType.DMA
    v = pltpu.VMEM
    scratch = [
        v((8, blk, width), BF16),
        v((PARTS, 16, tok, third), BF16),
        v((blk, width), BF16),
        v((blk, width), BF16),
        v((width, width), BF16),
        v((CUSTOMERS, RANK, width), BF16),
        v((CUSTOMERS, RANK, width), BF16),
        v((RANK, width), BF16),
        v((RANK, width), BF16),
        v((width, width), BF16),
        v((8, blk, width), BF16),
        v((2, blk, width), BF16),
        v((2, blk, width), BF16),
        v((2, 2, blk, width), BF16),
        v((4, 2, tok, wide), BF16),
        v((2, tok, wide), BF16),
        v((2, tok, wide), BF16),
        v((2, 2, tok, wide), BF16),
        v((PARTS, 4, piece, width), BF16),
        v((PARTS, 2, piece // 2, width), BF16),
        v((PARTS, 2, piece // 2, width), BF16),
        v((PARTS, 2, 2, piece // 2, width), BF16),
        v((4, RANK, 2 * LANES), BF16),
        v((4, RANK, 2 * LANES), BF16),
        v((2, 4, RANK, 2 * LANES), BF16),
        v((2, RANK, LANES), BF16),
        v((4, RANK, LANES), BF16),
        v((4, 4, RANK, LANES), BF16),
        v((2, 4, RANK, width), BF16),
        dma((8,)),
        dma((PARTS, 3)), dma((PARTS, 3)), dma((4, PARTS, 3)), dma((4, PARTS, 3)),
        dma((2, 4, 2)), dma((2, 4, 2)), dma((2, 4, 2)), dma((2, 4, 2)),
        dma((2,)), dma((2,)), dma((2, 2)), dma((2, 2)),
        dma((2,)), dma((2,)), dma((2, 2)), dma((2, 2)),
        dma((PARTS, 2)), dma((PARTS, 2)), dma((PARTS, 2)), dma((PARTS, 2)),
        dma((PARTS, 2)), dma((PARTS, 2)), dma((PARTS, 4)), dma((PARTS, 4)),
        dma((10, 3)), dma((10, 3)),
    ]
    gi, gw, li, lo = pl.pallas_call(
        kernel,
        out_shape=(
            pltpu.VMEM((tok, width), BF16),
            pltpu.VMEM((PARTS, 4, piece, width), BF16),
            pltpu.VMEM((CUSTOMERS, RANK, width), F32),
            pltpu.VMEM((CUSTOMERS, RANK, width), F32),
        ),
        in_specs=[hbm] * 6 + [pl.BlockSpec(memory_space=pltpu.SMEM)],
        out_specs=[pl.BlockSpec(memory_space=pltpu.VMEM)] * 4,
        scratch_shapes=scratch,
        compiler_params=pltpu.CompilerParams(
            collective_id=0, has_side_effects=True, vmem_limit_bytes=60 << 20
        ),
        name="mlp_backward",
    )(activations, cotangent, preact, weight, ain, aout, owner)
    return gi, gw.reshape(width, width), li, lo


def solution(mesh):
    placed = (
        P(("dp", "row"), "col"),
        P(("dp", "col"), "row"),
        P(("dp", "col"), "row"),
        P("col", "row"),
        P(None, None, "col"),
        P(None, None, "row"),
        P(),
    )
    return jax.shard_map(
        local,
        mesh=mesh,
        in_specs=placed,
        out_specs=(
            P(("dp", "row"), "col"),
            P("col", "row"),
            P(None, None, "col"),
            P(None, None, "row"),
        ),
        check_vma=False,
    )
```

```python
import functools

import jax
import jax.numpy as jnp
from jax import lax
from jax.experimental import pallas as pl
from jax.experimental.pallas import tpu as pltpu
from jax.sharding import PartitionSpec as P

MESH = pl.DeviceIdType.MESH
F32, BF16 = jnp.float32, jnp.bfloat16
SCALE = 2.0
CUSTOMERS = 3
RANK = 32
LANES = 128
PARTS = 3
DIRECT = 3


def gelu_slope(v):
    return 0.5 * (1.0 + lax.erf(v * 0.7071067811865476)) + v * jnp.exp(
        -0.5 * v * v
    ) * 0.3989422804014327


def kernel(
    x_in, cot_in, pre_in, w_in, ain_in, aout_in, owner,
    gi_out, gw_out, li_out, lo_out,
    gb, xb, cotv, prev, wv, av, bv, asel, bsel, weff, pb, ra, pa, rx, sz, rza, sza, rzf,
    wb, ryo, ryp, ryf, lgx, lgz, lgt, las, laz, lat, lg,
    load_sem, xz_s, xz_r, xx_s, xx_r, g_s, g_r, gk_s, gk_r, ra_s, ra_r, rx_s, rx_r,
    rza_s, rza_r, rzf_s, rzf_r, yo_s, yo_r, yd_s, yd_r, yp_s, yp_r, ag_s, ag_r, l_s, l_r,
):
    y, r, c = lax.axis_index("dp"), lax.axis_index("row"), lax.axis_index("col")
    i, j, o, k = r // 4, r % 4, c // 2, c % 2
    sign = 1 - 2 * k
    tok = xb.shape[2]
    blk = gb.shape[1]
    half = blk // 2
    width = gb.shape[2]
    wide = width // 2
    third = width // PARTS

    def wrap(v):
        return (v + 8) % 4

    def at_x(s):
        return (y, wrap(i + s) * 4 + j, c)

    def at_zhi(s):
        return (y, i * 4 + wrap(j + s), c)

    def at_zlo(s):
        return (y, r, wrap(o + s) * 2 + k)

    def at_y(s):
        return (wrap(y + s), r, c)

    sibling = (y, r, o * 2 + 1 - k)
    ways = (sign, -sign)

    def remote(src, dst, ss, rs, dev):
        return pltpu.make_async_remote_copy(
            src_ref=src, dst_ref=dst, send_sem=ss, recv_sem=rs, device_id=dev, device_id_type=MESH
        )

    loads = [
        pltpu.make_async_copy(a, b, load_sem.at[n])
        for n, (a, b) in enumerate(
            [(cot_in, cotv), (pre_in, prev), (w_in, wv), (ain_in, av), (aout_in, bv)]
            + [(x_in.at[:, pl.ds(t * third, third)], xb.at[t, r]) for t in range(PARTS)]
        )
    ]
    early = [loads[0], loads[1], *loads[5:]]
    late = loads[2:5]
    for cp in early:
        cp.start()
    barrier = pltpu.get_barrier_semaphore()
    for s in range(1, 4):
        for dev in (at_x(s), at_zhi(s), at_zlo(s), at_y(s)):
            pl.semaphore_signal(barrier, inc=1, device_id=dev, device_id_type=MESH)
    pl.semaphore_signal(barrier, inc=1, device_id=sibling, device_id_type=MESH)

    def nt(a, b):
        return lax.dot_general(a, b, (((1,), (1,)), ((), ())), preferred_element_type=F32)

    def lgx_send(s):
        return remote(lgx.at[i], lgx.at[i], l_s.at[0, s - 1], l_r.at[0, s - 1], at_x(s))

    def las_send():
        return remote(las.at[k], las.at[k], l_s.at[1, 0], l_r.at[1, 0], sibling)

    def lgz_send(s):
        return remote(lgz.at[j], lgz.at[j], l_s.at[2, s - 1], l_r.at[2, s - 1], at_zhi(s))

    def laz_send(s):
        return remote(laz.at[o], laz.at[o], l_s.at[3, s - 1], l_r.at[3, s - 1], at_zlo(s))

    def lgt_send(s):
        return remote(lgt.at[k, o], lgt.at[k, o], l_s.at[4, s - 1], l_r.at[4, s - 1], at_zlo(s))

    def lat_send(s):
        return remote(lat.at[i, j], lat.at[i, j], l_s.at[5, s - 1], l_r.at[5, s - 1], at_zhi(s))

    def lgt_sib():
        return remote(lgt.at[k], lgt.at[k], l_s.at[6, 0], l_r.at[6, 0], sibling)

    def lat_x(s):
        return remote(lat.at[i], lat.at[i], l_s.at[7, s - 1], l_r.at[7, s - 1], at_x(s))

    def lg_y(n, s):
        return remote(lg.at[n, y], lg.at[n, y], l_s.at[8 + n, s - 1], l_r.at[8 + n, s - 1], at_y(s))

    def xz_own(h, e):
        return remote(xb.at[h, r], xb.at[h, r], xz_s.at[h, e], xz_r.at[h, e], at_zhi(ways[e]))

    def xz_on(h):
        way = ways[h % 2]
        row = i * 4 + wrap(j - way)
        return remote(xb.at[h, row], xb.at[h, row], xz_s.at[h, 2], xz_r.at[h, 2], at_zhi(way))

    def xrow(ii, q):
        return wrap(ii) * 4 + wrap(j + (0, -sign, sign, 2)[q])

    def xx_own(q, h, e):
        row = xrow(i, q)
        return remote(xb.at[h, row], xb.at[h, row], xx_s.at[q, h, e], xx_r.at[q, h, e], at_x(ways[e]))

    def xx_on(q, h):
        way = ways[h % 2]
        row = xrow(i - way, q)
        return remote(xb.at[h, row], xb.at[h, row], xx_s.at[q, h, 2], xx_r.at[q, h, 2], at_x(way))

    def xx_direct(q, h):
        row = xrow(i, q)
        return remote(xb.at[h, row], xb.at[h, row], xx_s.at[q, h, 2], xx_r.at[q, h, 2], at_x(2))

    def xx_start(q, h):
        for e in range(2):
            xx_own(q, h, e).start()
        if q == DIRECT:
            xx_direct(q, h).start()

    def xx_forward(q, h):
        xx_own(q, h, h % 2).wait_recv()
        xx_on(q, h).start()

    def g_block(d, s):
        return (wrap(o - s) if d == 0 else wrap(o + s)) * 2 + k

    def g_hop(d, s, h):
        ref = gb.at[g_block(d, s), pl.ds(h * half, half)]
        return remote(ref, ref, g_s.at[d, s, h], g_r.at[d, s, h], at_zlo(1 - 2 * d))

    def g_sib(d, s, h):
        ref = gb.at[g_block(d, s), pl.ds(h * half, half)]
        return remote(ref, ref, gk_s.at[d, s, h], gk_r.at[d, s, h], sibling)

    def ra_send(kk):
        return remote(
            pb.at[wrap(i + 2) * 2 + kk], ra.at[kk], ra_s.at[kk], ra_r.at[kk], at_x(sign * (1 - 2 * kk))
        )

    def rx_send(kk):
        way = sign * (2 * kk - 1)
        return remote(
            pb.at[wrap(i + way) * 2 + kk], rx.at[1 - kk, kk], rx_s.at[1 - kk, kk], rx_r.at[1 - kk, kk], at_x(way)
        )

    def pa_send(kk):
        return remote(pa.at[kk], rx.at[kk, kk], rx_s.at[kk, kk], rx_r.at[kk, kk], at_x(ways[kk]))

    def part(oo, kk):
        b = oo * 2 + kk
        pb[b] = nt(gb[b], weff[...]).astype(BF16)

    def part_send(oo, kk):
        rel = wrap((oo - i) * sign)

        @pl.when(rel == 2)
        def _():
            ra_send(kk).start()

        @pl.when(rel == 3 - 2 * kk)
        def _():
            rx_send(kk).start()

    loads[0].wait()
    loads[1].wait()
    for cp in late:
        cp.start()
    for h in range(2):
        rows = pl.ds(h * half, half)
        v = prev[rows, :].astype(F32)
        gb[c, rows, :] = (cotv[rows, :].astype(F32) * gelu_slope(v)).astype(BF16)
    for t in range(PARTS):
        loads[5 + t].wait()
    with jax.named_scope("entry"):
        pl.semaphore_wait(barrier, 13)

    for h in range(2):

        @pl.when(o < 3)
        def _():
            g_hop(0, 0, h).start()

        @pl.when(o > 0)
        def _():
            g_hop(1, 0, h).start()

    for h in range(2):
        g_sib(0, 0, h).start()

    with jax.named_scope("fold"):
        loads[3].wait()
        loads[4].wait()
        mine = owner[y]
        a_sum = jnp.zeros(asel.shape, F32)
        b_sum = jnp.zeros(bsel.shape, F32)
        for n in range(CUSTOMERS):
            a_sum = a_sum + jnp.where(mine == n, av[n].astype(F32), 0.0)
            b_sum = b_sum + jnp.where(mine == n, bv[n].astype(F32), 0.0)
        asel[...] = a_sum.astype(BF16)
        bsel[...] = b_sum.astype(BF16)
        loads[2].wait()
        fold = lax.dot_general(
            asel[...], bsel[...], (((0,), (0,)), ((), ())), preferred_element_type=F32
        )
        weff[...] = (wv[...].astype(F32) + SCALE * fold).astype(BF16)

    with jax.named_scope("rank stage 1"):
        lgx[i] = jnp.zeros(lgx.shape[1:], BF16)
        for h in range(2):
            lgx[i, :, h * LANES : h * LANES + half] = nt(
                bsel[...], gb[c, h * half : (h + 1) * half, :]
            ).astype(BF16)
        las[k] = jnp.zeros(las.shape[1:], BF16)
        low = jnp.zeros((RANK, tok), F32)
        for t in range(PARTS):
            low = low + nt(asel[:, t * third : (t + 1) * third], xb[t, r])
        las[k, :, :tok] = low.astype(BF16)
        for s in range(1, 4):
            lgx_send(s).start()
        las_send().start()

    with jax.named_scope("own block"):
        part(o, k)
        part_send(o, k)
        for h in range(2):
            g_sib(0, 0, h).wait_recv()
        part(o, 1 - k)
        part_send(o, 1 - k)
        for t in range(PARTS):
            xx_start(0, t)

    def sum4(ref):
        return (ref[0].astype(F32) + ref[1].astype(F32)) + (ref[2].astype(F32) + ref[3].astype(F32))

    def g_step(s):
        here = (o >= s, o <= 3 - s)
        more = (o < 3, o > 0)
        for h in range(2):
            for d in range(2):

                @pl.when(here[d])
                def _():
                    g_hop(d, s - 1, h).wait_recv()

                @pl.when(jnp.logical_and(here[d], more[d]))
                def _():
                    g_hop(d, s, h).start()

                @pl.when(here[d])
                def _():
                    g_sib(d, s, h).start()

        for own in range(2):
            for d in range(2):
                oo = wrap(o - s) if d == 0 else wrap(o + s)

                @pl.when(here[d])
                def _():
                    kk = k if own == 0 else 1 - k
                    if own == 1:
                        for h in range(2):
                            g_sib(d, s, h).wait_recv()
                    part(oo, kk)
                    part_send(oo, kk)

    def pass_on(dist):
        with jax.named_scope(f"input sums x {dist}"):
            for kk in range(2):
                ii = wrap(i + ways[kk])

                @pl.when(jnp.logical_or(o - ii == dist, ii - o == dist))
                def _():
                    ra_send(kk).wait_recv()
                    pa[kk] = (pb[ii * 2 + kk].astype(F32) + ra[kk].astype(F32)).astype(BF16)
                    pa_send(kk).start()

    def act_z(t):
        with jax.named_scope(f"act z {t}"):
            for e in range(2):
                xz_own(t, e).wait_recv()
            xz_on(t).start()
            xx_start(1, t)
            xx_start(2, t)

    def act_z_last(t):
        with jax.named_scope(f"act z last {t}"):
            xz_on(t).wait_recv()
            xx_start(3, t)

    def act_x(q, t):
        with jax.named_scope(f"act x {q} {t}"):
            xx_forward(q, t)

    def xz_start(t):
        for e in range(2):
            xz_own(t, e).start()

    with jax.named_scope("gradients 1"):
        g_step(1)
    pass_on(0)
    for t in range(PARTS):
        act_x(0, t)
    with jax.named_scope("gradients 2"):
        g_step(2)
    pass_on(1)
    with jax.named_scope("gradients 3"):
        g_step(3)
    with jax.named_scope("gradients out"):
        for d in range(2):

            @pl.when((o == 2) if d == 0 else (o == 1))
            def _():
                for h in range(2):
                    g_hop(d, 2, h).wait_send()

    xz_start(0)
    pass_on(2)
    with jax.named_scope("rank stage 2"):
        for s in range(1, 4):
            lgx_send(s).wait_recv()
        lgz[j] = sum4(lgx).astype(BF16)
        las_send().wait_recv()
        laz[o] = (las[0].astype(F32) + las[1].astype(F32)).astype(BF16)
        for s in range(1, 4):
            lgz_send(s).start()
            laz_send(s).start()
    act_z(0)
    xz_start(1)
    xz_start(2)
    pass_on(3)
    act_x(1, 0)
    act_x(2, 0)
    act_z(1)
    act_z_last(0)
    with jax.named_scope("rank stage 3"):
        for s in range(1, 4):
            lgz_send(s).wait_recv()
            laz_send(s).wait_recv()
        lgt[k, o] = sum4(lgz).astype(BF16)
        lat[i, j] = sum4(laz).astype(BF16)
        for s in range(1, 4):
            lgt_send(s).start()
            lat_send(s).start()
    act_x(1, 1)
    act_x(2, 1)
    act_z(2)
    act_z_last(1)
    low_rows = wb.shape[2] // 2
    cuts = (pl.ds(0, low_rows), pl.ds(low_rows, low_rows))

    def yo_send(t, e):
        return remote(
            wb.at[t, wrap(y + 2), cuts[e]], ryo.at[t, e], yo_s.at[t, e], yo_r.at[t, e], at_y(ways[e])
        )

    def yd_send(t, e):
        return remote(
            wb.at[t, wrap(y + ways[e]), cuts[1 - e]], ryf.at[t, e, 1 - e], yd_s.at[t, e], yd_r.at[t, e], at_y(ways[e])
        )

    def yp_send(t, e):
        return remote(ryp.at[t, e], ryf.at[t, e, e], yp_s.at[t, e], yp_r.at[t, e], at_y(ways[e]))

    def pass_y(t):
        with jax.named_scope(f"y pass {t}"):
            for e in range(2):
                yo_send(t, e).wait_recv()
                own = wb[t, wrap(y + ways[e]), cuts[e], :].astype(F32)
                ryp[t, e] = (own + ryo[t, e].astype(F32)).astype(BF16)
                yp_send(t, e).start()

    gs = gb[...].reshape(8 * blk, width)

    def product(t):
        with jax.named_scope(f"product waits {t}"):
            for q in range(4):
                if q == DIRECT:
                    xx_own(q, t, t % 2).wait_recv()
                xx_own(q, t, 1 - t % 2).wait_recv()
                xx_on(q, t).wait_recv()
        with jax.named_scope(f"product {t}"):
            term = lax.dot_general(
                xb[t].reshape(16 * tok, third), gs, (((0,), (0,)), ((), ())), preferred_element_type=F32
            )
            wb[t] = term.astype(BF16).reshape(wb.shape[1:])
            for e in range(2):
                yo_send(t, e).start()
            for e in range(2):
                yd_send(t, e).start()

    def rza_send(h):
        return remote(sz.at[wrap(j + 2), h], rza.at[h], rza_s.at[h], rza_r.at[h], at_zhi(ways[h]))

    def rzf_send(h):
        way = ways[1 - h]
        return remote(
            sz.at[wrap(j + way), h], rzf.at[1 - h, h], rzf_s.at[1 - h, h], rzf_r.at[1 - h, h], at_zhi(way)
        )

    def sza_send(h):
        return remote(sza.at[h], rzf.at[h, h], rzf_s.at[h, h], rzf_r.at[h, h], at_zhi(ways[h]))

    def input_x():
        with jax.named_scope("input wait x"):
            for kk in range(2):
                pa_send(kk).wait_recv()
                rx_send(kk).wait_recv()
        for q in range(4):
            kk, rows = q // 2, pl.ds((q % 2) * tok, tok)
            total = pb[i * 2 + kk, rows, :].astype(F32)
            for e in range(2):
                total = total + rx[e, kk, rows, :].astype(F32)
            total = total.astype(BF16)
            sz[q, 0] = total[:, :wide]
            sz[q, 1] = total[:, wide:]
        for h in range(2):
            rza_send(h).start()

    def lo_part():
        with jax.named_scope("adapter out"):
            for s in range(1, 4):
                lat_x(s).wait_recv()
            lout = jnp.zeros((RANK, width), F32)
            for row in range(16):
                b, p = row // 2, row % 2
                lout = lout + jnp.dot(
                    lat[row // 4, row % 4, :, :tok],
                    gb[b, p * tok : (p + 1) * tok, :],
                    preferred_element_type=F32,
                )
            lg[1, y] = (SCALE * lout).astype(BF16)

    def li_part(t):
        with jax.named_scope(f"adapter in {t}"):
            if t == 0:
                lgt_sib().wait_recv()
            lin = jnp.zeros((RANK, third), F32)
            for row in range(16):
                b, p = row // 2, row % 2
                low = lgt[b % 2, b // 2, :, p * LANES : p * LANES + tok]
                lin = lin + jnp.dot(low, xb[t, row], preferred_element_type=F32)
            lg[0, y, :, t * third : (t + 1) * third] = (SCALE * lin).astype(BF16)

    def ag_own(t, e):
        return remote(gw_out.at[t, y], gw_out.at[t, y], ag_s.at[t, e], ag_r.at[t, e], at_y(ways[e]))

    def ag_on(t, e):
        ref = gw_out.at[t, wrap(y - ways[e]), cuts[e]]
        return remote(ref, ref, ag_s.at[t, 2 + e], ag_r.at[t, 2 + e], at_y(ways[e]))

    def sum_y(t):
        with jax.named_scope(f"y sum {t}"):
            for e in range(2):
                yd_send(t, e).wait_recv()
                yp_send(t, e).wait_recv()
            for h in range(2):
                total = wb[t, y, cuts[h], :].astype(F32)
                for e in range(2):
                    total = total + ryf[t, e, h].astype(F32)
                gw_out[t, y, cuts[h], :] = total.astype(BF16)
            for e in range(2):
                ag_own(t, e).start()

    def spread_y(t):
        with jax.named_scope(f"y spread {t}"):
            for e in range(2):
                ag_own(t, e).wait_recv()
                ag_on(t, e).start()

    def pass_z():
        with jax.named_scope("input sums z"):
            for h in range(2):
                rza_send(h).wait_recv()
                sza[h] = (sz[wrap(j + ways[h]), h].astype(F32) + rza[h].astype(F32)).astype(BF16)
                sza_send(h).start()

    product(0)
    act_x(1, 2)
    act_x(2, 2)
    act_z_last(2)
    input_x()
    with jax.named_scope("rank stage 4"):
        for s in range(1, 4):
            lgt_send(s).wait_recv()
            lat_send(s).wait_recv()
        lgt_sib().start()
        for s in range(1, 4):
            lat_x(s).start()
    pass_y(0)
    product(1)
    sum_y(0)
    for h in range(2):
        rzf_send(h).start()
    product(2)
    pass_y(1)
    pass_y(2)
    lo_part()
    for t in range(PARTS):
        li_part(t)
    sum_y(1)
    spread_y(0)
    pass_z()
    sum_y(2)
    for n in range(2):
        for s in range(1, 4):
            lg_y(n, s).start()
    spread_y(1)
    spread_y(2)

    with jax.named_scope("input wait z"):
        for h in range(2):
            rzf_send(h).wait_recv()
            sza_send(h).wait_recv()
    for h in range(2):
        total = sz[j, h].astype(F32)
        for e in range(2):
            total = total + rzf[e, h].astype(F32)
        gi_out[:, h * wide : (h + 1) * wide] = total.astype(BF16)
    with jax.named_scope("adapters wait y"):
        for s in range(1, 4):
            for n in range(2):
                lg_y(n, s).wait_recv()
    for n in range(CUSTOMERS):
        for m, ref in enumerate((li_out, lo_out)):
            acc = jnp.zeros((RANK, width), F32)
            for g in range(4):
                acc = acc + jnp.where(owner[g] == n, lg[m, g].astype(F32), 0.0)
            ref[n] = acc
    with jax.named_scope("y gather"):
        for t in range(PARTS):
            for e in range(2):
                ag_on(t, e).wait_recv()

    with jax.named_scope("sent"):
        for d in range(2):
            for s in range(4):
                sent = (o >= s) if d == 0 else (o <= 3 - s)
                if s < 2:

                    @pl.when(jnp.logical_and(sent, (o < 3) if d == 0 else (o > 0)))
                    def _():
                        for h in range(2):
                            g_hop(d, s, h).wait_send()

                if s > 0 or d == 0:

                    @pl.when(sent)
                    def _():
                        for h in range(2):
                            g_sib(d, s, h).wait_send()

        for t in range(PARTS):
            for e in range(2):
                xz_own(t, e).wait_send()
            xz_on(t).wait_send()
            for q in range(4):
                for e in range(2):
                    xx_own(q, t, e).wait_send()
                xx_on(q, t).wait_send()
            for e in range(2):
                yo_send(t, e).wait_send()
                yd_send(t, e).wait_send()
                yp_send(t, e).wait_send()
                ag_own(t, e).wait_send()
                ag_on(t, e).wait_send()
        for h in range(2):
            ra_send(h).wait_send()
            rx_send(h).wait_send()
            pa_send(h).wait_send()
            rza_send(h).wait_send()
            rzf_send(h).wait_send()
            sza_send(h).wait_send()
        las_send().wait_send()
        lgt_sib().wait_send()
        for s in range(1, 4):
            for small in (lgx_send, lgz_send, laz_send, lgt_send, lat_send, lat_x):
                small(s).wait_send()
            for n in range(2):
                lg_y(n, s).wait_send()


def local(activations, cotangent, preact, weight, ain, aout, owner):
    tok, width = activations.shape
    blk = cotangent.shape[0]
    wide = width // 2
    third = width // PARTS
    piece = third // 4
    hbm = pl.BlockSpec(memory_space=pltpu.HBM)
    dma = pltpu.SemaphoreType.DMA
    v = pltpu.VMEM
    scratch = [
        v((8, blk, width), BF16),
        v((PARTS, 16, tok, third), BF16),
        v((blk, width), BF16),
        v((blk, width), BF16),
        v((width, width), BF16),
        v((CUSTOMERS, RANK, width), BF16),
        v((CUSTOMERS, RANK, width), BF16),
        v((RANK, width), BF16),
        v((RANK, width), BF16),
        v((width, width), BF16),
        v((8, blk, width), BF16),
        v((2, blk, width), BF16),
        v((2, blk, width), BF16),
        v((2, 2, blk, width), BF16),
        v((4, 2, tok, wide), BF16),
        v((2, tok, wide), BF16),
        v((2, tok, wide), BF16),
        v((2, 2, tok, wide), BF16),
        v((PARTS, 4, piece, width), BF16),
        v((PARTS, 2, piece // 2, width), BF16),
        v((PARTS, 2, piece // 2, width), BF16),
        v((PARTS, 2, 2, piece // 2, width), BF16),
        v((4, RANK, 2 * LANES), BF16),
        v((4, RANK, 2 * LANES), BF16),
        v((2, 4, RANK, 2 * LANES), BF16),
        v((2, RANK, LANES), BF16),
        v((4, RANK, LANES), BF16),
        v((4, 4, RANK, LANES), BF16),
        v((2, 4, RANK, width), BF16),
        dma((8,)),
        dma((PARTS, 3)), dma((PARTS, 3)), dma((4, PARTS, 3)), dma((4, PARTS, 3)),
        dma((2, 4, 2)), dma((2, 4, 2)), dma((2, 4, 2)), dma((2, 4, 2)),
        dma((2,)), dma((2,)), dma((2, 2)), dma((2, 2)),
        dma((2,)), dma((2,)), dma((2, 2)), dma((2, 2)),
        dma((PARTS, 2)), dma((PARTS, 2)), dma((PARTS, 2)), dma((PARTS, 2)),
        dma((PARTS, 2)), dma((PARTS, 2)), dma((PARTS, 4)), dma((PARTS, 4)),
        dma((10, 3)), dma((10, 3)),
    ]
    gi, gw, li, lo = pl.pallas_call(
        kernel,
        out_shape=(
            pltpu.VMEM((tok, width), BF16),
            pltpu.VMEM((PARTS, 4, piece, width), BF16),
            pltpu.VMEM((CUSTOMERS, RANK, width), F32),
            pltpu.VMEM((CUSTOMERS, RANK, width), F32),
        ),
        in_specs=[hbm] * 6 + [pl.BlockSpec(memory_space=pltpu.SMEM)],
        out_specs=[pl.BlockSpec(memory_space=pltpu.VMEM)] * 4,
        scratch_shapes=scratch,
        compiler_params=pltpu.CompilerParams(
            collective_id=0, has_side_effects=True, vmem_limit_bytes=60 << 20
        ),
        name="mlp_backward",
    )(activations, cotangent, preact, weight, ain, aout, owner)
    return gi, gw.reshape(width, width), li, lo


def solution(mesh):
    placed = (
        P(("dp", "row"), "col"),
        P(("dp", "col"), "row"),
        P(("dp", "col"), "row"),
        P("col", "row"),
        P(None, None, "col"),
        P(None, None, "row"),
        P(),
    )
    return jax.shard_map(
        local,
        mesh=mesh,
        in_specs=placed,
        out_specs=(
            P(("dp", "row"), "col"),
            P("col", "row"),
            P(None, None, "col"),
            P(None, None, "row"),
        ),
        check_vma=False,
    )
```

```python
import functools

import jax
import jax.numpy as jnp
from jax import lax
from jax.experimental import pallas as pl
from jax.experimental.pallas import tpu as pltpu
from jax.sharding import PartitionSpec as P

MESH = pl.DeviceIdType.MESH
F32, BF16 = jnp.float32, jnp.bfloat16
SCALE = 2.0
CUSTOMERS = 3
RANK = 32
LANES = 128
PARTS = 3
DIRECT = 3


def gelu_slope(v):
    return 0.5 * (1.0 + lax.erf(v * 0.7071067811865476)) + v * jnp.exp(
        -0.5 * v * v
    ) * 0.3989422804014327


def kernel(
    x_in, cot_in, pre_in, w_in, ain_in, aout_in, owner,
    gi_out, gw_out, li_out, lo_out,
    gb, xb, cotv, prev, wv, av, bv, asel, bsel, weff, pb, ra, pa, rx, sz, rza, sza, rzf,
    wb, ryo, ryp, ryf, lgx, lgz, lgt, las, laz, lat, lg,
    load_sem, xz_s, xz_r, xx_s, xx_r, g_s, g_r, gk_s, gk_r, ra_s, ra_r, rx_s, rx_r,
    rza_s, rza_r, rzf_s, rzf_r, yo_s, yo_r, yd_s, yd_r, yp_s, yp_r, ag_s, ag_r, l_s, l_r,
):
    y, r, c = lax.axis_index("dp"), lax.axis_index("row"), lax.axis_index("col")
    i, j, o, k = r // 4, r % 4, c // 2, c % 2
    sign = 1 - 2 * k
    tok = xb.shape[2]
    blk = gb.shape[1]
    half = blk // 2
    width = gb.shape[2]
    wide = width // 2
    third = width // PARTS

    def wrap(v):
        return (v + 8) % 4

    def at_x(s):
        return (y, wrap(i + s) * 4 + j, c)

    def at_zhi(s):
        return (y, i * 4 + wrap(j + s), c)

    def at_zlo(s):
        return (y, r, wrap(o + s) * 2 + k)

    def at_y(s):
        return (wrap(y + s), r, c)

    sibling = (y, r, o * 2 + 1 - k)
    ways = (sign, -sign)

    def remote(src, dst, ss, rs, dev):
        return pltpu.make_async_remote_copy(
            src_ref=src, dst_ref=dst, send_sem=ss, recv_sem=rs, device_id=dev, device_id_type=MESH
        )

    loads = [
        pltpu.make_async_copy(a, b, load_sem.at[n])
        for n, (a, b) in enumerate(
            [(cot_in, cotv), (pre_in, prev), (w_in, wv), (ain_in, av), (aout_in, bv)]
            + [(x_in.at[:, pl.ds(t * third, third)], xb.at[t, r]) for t in range(PARTS)]
        )
    ]
    early = [loads[0], loads[1], *loads[5:]]
    late = loads[2:5]
    for cp in early:
        cp.start()
    barrier = pltpu.get_barrier_semaphore()
    for s in range(1, 4):
        for dev in (at_x(s), at_zhi(s), at_zlo(s), at_y(s)):
            pl.semaphore_signal(barrier, inc=1, device_id=dev, device_id_type=MESH)
    pl.semaphore_signal(barrier, inc=1, device_id=sibling, device_id_type=MESH)

    def nt(a, b):
        return lax.dot_general(a, b, (((1,), (1,)), ((), ())), preferred_element_type=F32)

    def lgx_send(s):
        return remote(lgx.at[i], lgx.at[i], l_s.at[0, s - 1], l_r.at[0, s - 1], at_x(s))

    def las_send():
        return remote(las.at[k], las.at[k], l_s.at[1, 0], l_r.at[1, 0], sibling)

    def lgz_send(s):
        return remote(lgz.at[j], lgz.at[j], l_s.at[2, s - 1], l_r.at[2, s - 1], at_zhi(s))

    def laz_send(s):
        return remote(laz.at[o], laz.at[o], l_s.at[3, s - 1], l_r.at[3, s - 1], at_zlo(s))

    def lgt_send(s):
        return remote(lgt.at[k, o], lgt.at[k, o], l_s.at[4, s - 1], l_r.at[4, s - 1], at_zlo(s))

    def lat_send(s):
        return remote(lat.at[i, j], lat.at[i, j], l_s.at[5, s - 1], l_r.at[5, s - 1], at_zhi(s))

    def lgt_sib():
        return remote(lgt.at[k], lgt.at[k], l_s.at[6, 0], l_r.at[6, 0], sibling)

    def lat_x(s):
        return remote(lat.at[i], lat.at[i], l_s.at[7, s - 1], l_r.at[7, s - 1], at_x(s))

    def lg_y(n, s):
        return remote(lg.at[n, y], lg.at[n, y], l_s.at[8 + n, s - 1], l_r.at[8 + n, s - 1], at_y(s))

    def xz_own(h, e):
        return remote(xb.at[h, r], xb.at[h, r], xz_s.at[h, e], xz_r.at[h, e], at_zhi(ways[e]))

    def xz_on(h):
        way = ways[h % 2]
        row = i * 4 + wrap(j - way)
        return remote(xb.at[h, row], xb.at[h, row], xz_s.at[h, 2], xz_r.at[h, 2], at_zhi(way))

    def xrow(ii, q):
        return wrap(ii) * 4 + wrap(j + (0, -sign, sign, 2)[q])

    def xx_own(q, h, e):
        row = xrow(i, q)
        return remote(xb.at[h, row], xb.at[h, row], xx_s.at[q, h, e], xx_r.at[q, h, e], at_x(ways[e]))

    def xx_on(q, h):
        way = ways[h % 2]
        row = xrow(i - way, q)
        return remote(xb.at[h, row], xb.at[h, row], xx_s.at[q, h, 2], xx_r.at[q, h, 2], at_x(way))

    def xx_direct(q, h):
        row = xrow(i, q)
        return remote(xb.at[h, row], xb.at[h, row], xx_s.at[q, h, 2], xx_r.at[q, h, 2], at_x(2))

    def xx_start(q, h):
        for e in range(2):
            xx_own(q, h, e).start()
        if q == DIRECT:
            xx_direct(q, h).start()

    def xx_forward(q, h):
        xx_own(q, h, h % 2).wait_recv()
        xx_on(q, h).start()

    def g_block(d, s):
        return (wrap(o - s) if d == 0 else wrap(o + s)) * 2 + k

    def g_hop(d, s, h):
        ref = gb.at[g_block(d, s), pl.ds(h * half, half)]
        return remote(ref, ref, g_s.at[d, s, h], g_r.at[d, s, h], at_zlo(1 - 2 * d))

    def g_sib(d, s, h):
        ref = gb.at[g_block(d, s), pl.ds(h * half, half)]
        return remote(ref, ref, gk_s.at[d, s, h], gk_r.at[d, s, h], sibling)

    def ra_send(kk):
        return remote(
            pb.at[wrap(i + 2) * 2 + kk], ra.at[kk], ra_s.at[kk], ra_r.at[kk], at_x(sign * (1 - 2 * kk))
        )

    def rx_send(kk):
        way = sign * (2 * kk - 1)
        return remote(
            pb.at[wrap(i + way) * 2 + kk], rx.at[1 - kk, kk], rx_s.at[1 - kk, kk], rx_r.at[1 - kk, kk], at_x(way)
        )

    def pa_send(kk):
        return remote(pa.at[kk], rx.at[kk, kk], rx_s.at[kk, kk], rx_r.at[kk, kk], at_x(ways[kk]))

    def part(oo, kk):
        b = oo * 2 + kk
        pb[b] = nt(gb[b], weff[...]).astype(BF16)

    def part_send(oo, kk):
        rel = wrap((oo - i) * sign)

        @pl.when(rel == 2)
        def _():
            ra_send(kk).start()

        @pl.when(rel == 3 - 2 * kk)
        def _():
            rx_send(kk).start()

    loads[0].wait()
    loads[1].wait()
    for cp in late:
        cp.start()
    for h in range(2):
        rows = pl.ds(h * half, half)
        v = prev[rows, :].astype(F32)
        gb[c, rows, :] = (cotv[rows, :].astype(F32) * gelu_slope(v)).astype(BF16)
    for t in range(PARTS):
        loads[5 + t].wait()
    with jax.named_scope("entry"):
        pl.semaphore_wait(barrier, 13)

    for h in range(2):

        @pl.when(o < 3)
        def _():
            g_hop(0, 0, h).start()

        @pl.when(o > 0)
        def _():
            g_hop(1, 0, h).start()

    for h in range(2):
        g_sib(0, 0, h).start()

    with jax.named_scope("fold"):
        loads[3].wait()
        loads[4].wait()
        mine = owner[y]
        a_sum = jnp.zeros(asel.shape, F32)
        b_sum = jnp.zeros(bsel.shape, F32)
        for n in range(CUSTOMERS):
            a_sum = a_sum + jnp.where(mine == n, av[n].astype(F32), 0.0)
            b_sum = b_sum + jnp.where(mine == n, bv[n].astype(F32), 0.0)
        asel[...] = a_sum.astype(BF16)
        bsel[...] = b_sum.astype(BF16)
        loads[2].wait()
        fold = lax.dot_general(
            asel[...], bsel[...], (((0,), (0,)), ((), ())), preferred_element_type=F32
        )
        weff[...] = (wv[...].astype(F32) + SCALE * fold).astype(BF16)

    with jax.named_scope("rank stage 1"):
        lgx[i] = jnp.zeros(lgx.shape[1:], BF16)
        for h in range(2):
            lgx[i, :, h * LANES : h * LANES + half] = nt(
                bsel[...], gb[c, h * half : (h + 1) * half, :]
            ).astype(BF16)
        las[k] = jnp.zeros(las.shape[1:], BF16)
        low = jnp.zeros((RANK, tok), F32)
        for t in range(PARTS):
            low = low + nt(asel[:, t * third : (t + 1) * third], xb[t, r])
        las[k, :, :tok] = low.astype(BF16)
        for s in range(1, 4):
            lgx_send(s).start()
        las_send().start()

    with jax.named_scope("own block"):
        part(o, k)
        part_send(o, k)
        for h in range(2):
            g_sib(0, 0, h).wait_recv()
        part(o, 1 - k)
        part_send(o, 1 - k)
        for t in range(PARTS):
            xx_start(0, t)

    def sum4(ref):
        return (ref[0].astype(F32) + ref[1].astype(F32)) + (ref[2].astype(F32) + ref[3].astype(F32))

    def g_step(s):
        here = (o >= s, o <= 3 - s)
        more = (o < 3, o > 0)
        for h in range(2):
            for d in range(2):

                @pl.when(here[d])
                def _():
                    g_hop(d, s - 1, h).wait_recv()

                @pl.when(jnp.logical_and(here[d], more[d]))
                def _():
                    g_hop(d, s, h).start()

                @pl.when(here[d])
                def _():
                    g_sib(d, s, h).start()

        for own in range(2):
            for d in range(2):
                oo = wrap(o - s) if d == 0 else wrap(o + s)

                @pl.when(here[d])
                def _():
                    kk = k if own == 0 else 1 - k
                    if own == 1:
                        for h in range(2):
                            g_sib(d, s, h).wait_recv()
                    part(oo, kk)
                    part_send(oo, kk)

    def pass_on(dist):
        with jax.named_scope(f"input sums x {dist}"):
            for kk in range(2):
                ii = wrap(i + ways[kk])

                @pl.when(jnp.logical_or(o - ii == dist, ii - o == dist))
                def _():
                    ra_send(kk).wait_recv()
                    pa[kk] = (pb[ii * 2 + kk].astype(F32) + ra[kk].astype(F32)).astype(BF16)
                    pa_send(kk).start()

    def act_z(t):
        with jax.named_scope(f"act z {t}"):
            for e in range(2):
                xz_own(t, e).wait_recv()
            xz_on(t).start()
            xx_start(1, t)
            xx_start(2, t)

    def act_z_last(t):
        with jax.named_scope(f"act z last {t}"):
            xz_on(t).wait_recv()
            xx_start(3, t)

    def act_x(q, t):
        with jax.named_scope(f"act x {q} {t}"):
            xx_forward(q, t)

    def xz_start(t):
        for e in range(2):
            xz_own(t, e).start()

    with jax.named_scope("gradients 1"):
        g_step(1)
    pass_on(0)
    for t in range(PARTS):
        act_x(0, t)
    with jax.named_scope("gradients 2"):
        g_step(2)
    pass_on(1)
    with jax.named_scope("gradients 3"):
        g_step(3)
    with jax.named_scope("gradients out"):
        for d in range(2):

            @pl.when((o == 2) if d == 0 else (o == 1))
            def _():
                for h in range(2):
                    g_hop(d, 2, h).wait_send()

    xz_start(0)
    pass_on(2)
    with jax.named_scope("rank stage 2"):
        for s in range(1, 4):
            lgx_send(s).wait_recv()
        lgz[j] = sum4(lgx).astype(BF16)
        las_send().wait_recv()
        laz[o] = (las[0].astype(F32) + las[1].astype(F32)).astype(BF16)
        for s in range(1, 4):
            lgz_send(s).start()
            laz_send(s).start()
    act_z(0)
    xz_start(1)
    xz_start(2)
    pass_on(3)
    act_x(1, 0)
    act_x(2, 0)
    act_z(1)
    act_z_last(0)
    with jax.named_scope("rank stage 3"):
        for s in range(1, 4):
            lgz_send(s).wait_recv()
            laz_send(s).wait_recv()
        lgt[k, o] = sum4(lgz).astype(BF16)
        lat[i, j] = sum4(laz).astype(BF16)
        for s in range(1, 4):
            lgt_send(s).start()
            lat_send(s).start()
    act_x(1, 1)
    act_x(2, 1)
    act_z(2)
    act_z_last(1)
    low_rows = wb.shape[2] // 2
    cuts = (pl.ds(0, low_rows), pl.ds(low_rows, low_rows))

    def yo_send(t, e):
        return remote(
            wb.at[t, wrap(y + 2), cuts[e]], ryo.at[t, e], yo_s.at[t, e], yo_r.at[t, e], at_y(ways[e])
        )

    def yd_send(t, e):
        return remote(
            wb.at[t, wrap(y + ways[e]), cuts[1 - e]], ryf.at[t, e, 1 - e], yd_s.at[t, e], yd_r.at[t, e], at_y(ways[e])
        )

    def yp_send(t, e):
        return remote(ryp.at[t, e], ryf.at[t, e, e], yp_s.at[t, e], yp_r.at[t, e], at_y(ways[e]))

    def pass_y(t):
        with jax.named_scope(f"y pass {t}"):
            for e in range(2):
                yo_send(t, e).wait_recv()
                own = wb[t, wrap(y + ways[e]), cuts[e], :].astype(F32)
                ryp[t, e] = (own + ryo[t, e].astype(F32)).astype(BF16)
                yp_send(t, e).start()

    gs = gb[...].reshape(8 * blk, width)

    def product(t):
        with jax.named_scope(f"product waits {t}"):
            for q in range(4):
                if q == DIRECT:
                    xx_own(q, t, t % 2).wait_recv()
                xx_own(q, t, 1 - t % 2).wait_recv()
                xx_on(q, t).wait_recv()
        with jax.named_scope(f"product {t}"):
            term = lax.dot_general(
                xb[t].reshape(16 * tok, third), gs, (((0,), (0,)), ((), ())), preferred_element_type=F32
            )
            wb[t] = term.astype(BF16).reshape(wb.shape[1:])
            for e in range(2):
                yo_send(t, e).start()
            for e in range(2):
                yd_send(t, e).start()

    def rza_send(h):
        return remote(sz.at[wrap(j + 2), h], rza.at[h], rza_s.at[h], rza_r.at[h], at_zhi(ways[h]))

    def rzf_send(h):
        way = ways[1 - h]
        return remote(
            sz.at[wrap(j + way), h], rzf.at[1 - h, h], rzf_s.at[1 - h, h], rzf_r.at[1 - h, h], at_zhi(way)
        )

    def sza_send(h):
        return remote(sza.at[h], rzf.at[h, h], rzf_s.at[h, h], rzf_r.at[h, h], at_zhi(ways[h]))

    def input_x():
        with jax.named_scope("input wait x"):
            for kk in range(2):
                pa_send(kk).wait_recv()
                rx_send(kk).wait_recv()
        for q in range(4):
            kk, rows = q // 2, pl.ds((q % 2) * tok, tok)
            total = pb[i * 2 + kk, rows, :].astype(F32)
            for e in range(2):
                total = total + rx[e, kk, rows, :].astype(F32)
            total = total.astype(BF16)
            sz[q, 0] = total[:, :wide]
            sz[q, 1] = total[:, wide:]
        for h in range(2):
            rza_send(h).start()

    def lo_part():
        with jax.named_scope("adapter out"):
            for s in range(1, 4):
                lat_x(s).wait_recv()
            lout = jnp.zeros((RANK, width), F32)
            for row in range(16):
                b, p = row // 2, row % 2
                lout = lout + jnp.dot(
                    lat[row // 4, row % 4, :, :tok],
                    gb[b, p * tok : (p + 1) * tok, :],
                    preferred_element_type=F32,
                )
            lg[1, y] = (SCALE * lout).astype(BF16)

    def li_part(t):
        with jax.named_scope(f"adapter in {t}"):
            if t == 0:
                lgt_sib().wait_recv()
            lin = jnp.zeros((RANK, third), F32)
            for row in range(16):
                b, p = row // 2, row % 2
                low = lgt[b % 2, b // 2, :, p * LANES : p * LANES + tok]
                lin = lin + jnp.dot(low, xb[t, row], preferred_element_type=F32)
            lg[0, y, :, t * third : (t + 1) * third] = (SCALE * lin).astype(BF16)

    def ag_own(t, e):
        return remote(gw_out.at[t, y], gw_out.at[t, y], ag_s.at[t, e], ag_r.at[t, e], at_y(ways[e]))

    def ag_on(t, e):
        ref = gw_out.at[t, wrap(y - ways[e]), cuts[e]]
        return remote(ref, ref, ag_s.at[t, 2 + e], ag_r.at[t, 2 + e], at_y(ways[e]))

    def sum_y(t):
        with jax.named_scope(f"y sum {t}"):
            for e in range(2):
                yd_send(t, e).wait_recv()
                yp_send(t, e).wait_recv()
            for h in range(2):
                total = wb[t, y, cuts[h], :].astype(F32)
                for e in range(2):
                    total = total + ryf[t, e, h].astype(F32)
                gw_out[t, y, cuts[h], :] = total.astype(BF16)
            for e in range(2):
                ag_own(t, e).start()

    def spread_y(t):
        with jax.named_scope(f"y spread {t}"):
            for e in range(2):
                ag_own(t, e).wait_recv()
                ag_on(t, e).start()

    def pass_z():
        with jax.named_scope("input sums z"):
            for h in range(2):
                rza_send(h).wait_recv()
                sza[h] = (sz[wrap(j + ways[h]), h].astype(F32) + rza[h].astype(F32)).astype(BF16)
                sza_send(h).start()

    product(0)
    act_x(1, 2)
    act_x(2, 2)
    act_z_last(2)
    input_x()
    with jax.named_scope("rank stage 4"):
        for s in range(1, 4):
            lgt_send(s).wait_recv()
            lat_send(s).wait_recv()
        lgt_sib().start()
        for s in range(1, 4):
            lat_x(s).start()
    pass_y(0)
    product(1)
    sum_y(0)
    for h in range(2):
        rzf_send(h).start()
    product(2)
    pass_y(1)
    pass_y(2)
    lo_part()
    for t in range(PARTS):
        li_part(t)
    sum_y(1)
    spread_y(0)
    pass_z()
    sum_y(2)
    for n in range(2):
        for s in range(1, 4):
            lg_y(n, s).start()
    spread_y(1)
    spread_y(2)

    with jax.named_scope("input wait z"):
        for h in range(2):
            rzf_send(h).wait_recv()
            sza_send(h).wait_recv()
    for h in range(2):
        total = sz[j, h].astype(F32)
        for e in range(2):
            total = total + rzf[e, h].astype(F32)
        gi_out[:, h * wide : (h + 1) * wide] = total.astype(BF16)
    with jax.named_scope("adapters wait y"):
        for s in range(1, 4):
            for n in range(2):
                lg_y(n, s).wait_recv()
    for n in range(CUSTOMERS):
        for m, ref in enumerate((li_out, lo_out)):
            acc = jnp.zeros((RANK, width), F32)
            for g in range(4):
                acc = acc + jnp.where(owner[g] == n, lg[m, g].astype(F32), 0.0)
            ref[n] = acc
    with jax.named_scope("y gather"):
        for t in range(PARTS):
            for e in range(2):
                ag_on(t, e).wait_recv()

    with jax.named_scope("sent"):
        for d in range(2):
            for s in range(4):
                sent = (o >= s) if d == 0 else (o <= 3 - s)
                if s < 2:

                    @pl.when(jnp.logical_and(sent, (o < 3) if d == 0 else (o > 0)))
                    def _():
                        for h in range(2):
                            g_hop(d, s, h).wait_send()

                if s > 0 or d == 0:

                    @pl.when(sent)
                    def _():
                        for h in range(2):
                            g_sib(d, s, h).wait_send()

        for t in range(PARTS):
            for e in range(2):
                xz_own(t, e).wait_send()
            xz_on(t).wait_send()
            for q in range(4):
                for e in range(2):
                    xx_own(q, t, e).wait_send()
                xx_on(q, t).wait_send()
            for e in range(2):
                yo_send(t, e).wait_send()
                yd_send(t, e).wait_send()
                yp_send(t, e).wait_send()
                ag_own(t, e).wait_send()
                ag_on(t, e).wait_send()
        for h in range(2):
            ra_send(h).wait_send()
            rx_send(h).wait_send()
            pa_send(h).wait_send()
            rza_send(h).wait_send()
            rzf_send(h).wait_send()
            sza_send(h).wait_send()
        las_send().wait_send()
        lgt_sib().wait_send()
        for s in range(1, 4):
            for small in (lgx_send, lgz_send, laz_send, lgt_send, lat_send, lat_x):
                small(s).wait_send()
            for n in range(2):
                lg_y(n, s).wait_send()


def store_kernel(*refs):
    copies = [pltpu.make_async_copy(refs[n], refs[4 + n], refs[8].at[n]) for n in range(4)]
    for cp in copies:
        cp.start()
    for cp in copies:
        cp.wait()


def local(activations, cotangent, preact, weight, ain, aout, owner):
    tok, width = activations.shape
    blk = cotangent.shape[0]
    wide = width // 2
    third = width // PARTS
    piece = third // 4
    hbm = pl.BlockSpec(memory_space=pltpu.HBM)
    dma = pltpu.SemaphoreType.DMA
    v = pltpu.VMEM
    scratch = [
        v((8, blk, width), BF16),
        v((PARTS, 16, tok, third), BF16),
        v((blk, width), BF16),
        v((blk, width), BF16),
        v((width, width), BF16),
        v((CUSTOMERS, RANK, width), BF16),
        v((CUSTOMERS, RANK, width), BF16),
        v((RANK, width), BF16),
        v((RANK, width), BF16),
        v((width, width), BF16),
        v((8, blk, width), BF16),
        v((2, blk, width), BF16),
        v((2, blk, width), BF16),
        v((2, 2, blk, width), BF16),
        v((4, 2, tok, wide), BF16),
        v((2, tok, wide), BF16),
        v((2, tok, wide), BF16),
        v((2, 2, tok, wide), BF16),
        v((PARTS, 4, piece, width), BF16),
        v((PARTS, 2, piece // 2, width), BF16),
        v((PARTS, 2, piece // 2, width), BF16),
        v((PARTS, 2, 2, piece // 2, width), BF16),
        v((4, RANK, 2 * LANES), BF16),
        v((4, RANK, 2 * LANES), BF16),
        v((2, 4, RANK, 2 * LANES), BF16),
        v((2, RANK, LANES), BF16),
        v((4, RANK, LANES), BF16),
        v((4, 4, RANK, LANES), BF16),
        v((2, 4, RANK, width), BF16),
        dma((8,)),
        dma((PARTS, 3)), dma((PARTS, 3)), dma((4, PARTS, 3)), dma((4, PARTS, 3)),
        dma((2, 4, 2)), dma((2, 4, 2)), dma((2, 4, 2)), dma((2, 4, 2)),
        dma((2,)), dma((2,)), dma((2, 2)), dma((2, 2)),
        dma((2,)), dma((2,)), dma((2, 2)), dma((2, 2)),
        dma((PARTS, 2)), dma((PARTS, 2)), dma((PARTS, 2)), dma((PARTS, 2)),
        dma((PARTS, 2)), dma((PARTS, 2)), dma((PARTS, 4)), dma((PARTS, 4)),
        dma((10, 3)), dma((10, 3)),
    ]
    gi, gw, li, lo = pl.pallas_call(
        kernel,
        out_shape=(
            pltpu.VMEM((tok, width), BF16),
            pltpu.VMEM((PARTS, 4, piece, width), BF16),
            pltpu.VMEM((CUSTOMERS, RANK, width), F32),
            pltpu.VMEM((CUSTOMERS, RANK, width), F32),
        ),
        in_specs=[hbm] * 6 + [pl.BlockSpec(memory_space=pltpu.SMEM)],
        out_specs=[pl.BlockSpec(memory_space=pltpu.VMEM)] * 4,
        scratch_shapes=scratch,
        compiler_params=pltpu.CompilerParams(
            collective_id=0, has_side_effects=True, vmem_limit_bytes=60 << 20
        ),
        name="mlp_backward",
    )(activations, cotangent, preact, weight, ain, aout, owner)
    held = [pltpu.with_memory_space_constraint(v, pltpu.VMEM) for v in (gi, gw, li, lo)]
    gi, gw, li, lo = pl.pallas_call(
        store_kernel,
        out_shape=(
            jax.ShapeDtypeStruct((tok, width), BF16),
            jax.ShapeDtypeStruct((PARTS, 4, piece, width), BF16),
            jax.ShapeDtypeStruct((CUSTOMERS, RANK, width), F32),
            jax.ShapeDtypeStruct((CUSTOMERS, RANK, width), F32),
        ),
        in_specs=[pl.BlockSpec(memory_space=pltpu.VMEM)] * 4,
        out_specs=[hbm] * 4,
        scratch_shapes=[dma((4,))],
        name="store_results",
    )(*held)
    return gi, gw.reshape(width, width), li, lo


def solution(mesh):
    placed = (
        P(("dp", "row"), "col"),
        P(("dp", "col"), "row"),
        P(("dp", "col"), "row"),
        P("col", "row"),
        P(None, None, "col"),
        P(None, None, "row"),
        P(),
    )
    return jax.shard_map(
        local,
        mesh=mesh,
        in_specs=placed,
        out_specs=(
            P(("dp", "row"), "col"),
            P("col", "row"),
            P(None, None, "col"),
            P(None, None, "row"),
        ),
        check_vma=False,
    )
```
